128 devices in a mesh: seq: 16 (over x_hi, z, core), head: 8 (over y, x_lo).
Axes of the slice: x: 4 (x_hi: 2, x_lo: 2; x = x_hi * 2 + x_lo), y: 4, z: 4, core: 2. Of those that a mesh axis runs over, the one named last changes fastest.
Arguments:
- hidden_low: bfloat16 [2048, 4096], P('seq'), may hold values from -2 to 2
- query_low: bfloat16 [2048, 4096], P('seq', 'head'), may hold values from -48 to 48
- key_low: bfloat16 [2048, 4096], P('seq', 'head'), may hold values from -10 to 10
- value_low: bfloat16 [2048, 4096], P('seq', 'head'), may hold values from -6 to 6
- out_weight: bfloat16 [4096, 4096], P('head'), may hold values from -0.09375 to 0.09375
- latent_weight: bfloat16 [4096, 128], replicated, may hold values from -0.09375 to 0.09375
- conv_first: bfloat16 [3, 3, 3, 128, 512], replicated, may hold values from -0.109375 to 0.109375
- bias_first: float32 [512], replicated, may hold values from -3 to 3
- conv_second: bfloat16 [512, 512], replicated, may hold values from -0.25 to 0.25
- bias_second: float32 [512], replicated, may hold values from -3 to 3
- query_weight: bfloat16 [128, 4096], replicated, may hold values from -0.36 to 0.36
- key_weight: bfloat16 [128, 4096], replicated, may hold values from -0.36 to 0.36
- value_weight: bfloat16 [128, 4096], replicated, may hold values from -0.5 to 0.5
- query_gain: float32 [4096], replicated, may hold values from 0.1 to 6.3
- key_gain: float32 [4096], replicated, may hold values from 0.1 to 6.3
Outputs:
- hires_attention: bfloat16 [8192, 4096], P('seq', 'head')
- upsampled: bfloat16 [8192, 128], P(('seq', 'head'))
The draws below stay inside these ranges and needn't reach their ends.
All inputs are finite; a program needn't handle non-finite values.
Results may differ from the reference program's by a relative error of at most 0.04.
Values may be sent and summed in bfloat16 or wider, within the bound.
No kernel may reach another device: no remote copies, remote signals or barrier semaphores. Data moves between devices by JAX's collectives and lax.ppermute only.
A program may use at most 192 MiB of HBM per device.

```python
import math
import jax
import jax.numpy as jnp
from jax import lax

D = 4096
HEADS = 32
HD = 128
C = 128
MID = 512
H_LO = 4
W_LO = 32
TOKENS_LO = 2048
TOKENS_HI = 8192
N_SEQ = 16


def shared_normals(key):
    first_key, second_key = jax.random.split(key)
    query_base = jax.random.truncated_normal(first_key, -4.0, 4.0, (TOKENS_LO, D), jnp.float32)
    key_base = jax.random.truncated_normal(second_key, -4.0, 4.0, (TOKENS_LO, D), jnp.float32)
    return (query_base, key_base)


def projection_weight(key):
    weight = jax.random.truncated_normal(key, -4.0, 4.0, (C, D), jnp.float32) * 0.09
    return weight.astype(jnp.bfloat16)


def norm_gain(key):
    gain = jnp.exp(jax.random.uniform(key, (D,), jnp.float32, -1.1, 1.1))
    return gain.astype(jnp.float32)


def draw_query_low(key, part):
    query_base, key_base = shared_normals(key)
    return query_base.astype(jnp.bfloat16)


def draw_key_low(key, part):
    query_base, key_base = shared_normals(key)
    return key_base.astype(jnp.bfloat16)


def draw_query_weight(key, part):
    key = jax.random.fold_in(key, 7)
    return projection_weight(key)


def draw_key_weight(key, part):
    key = jax.random.fold_in(key, 9)
    return projection_weight(key)


def draw_query_gain(key, part):
    key = jax.random.fold_in(key, 13)
    return norm_gain(key)


def draw_key_gain(key, part):
    key = jax.random.fold_in(key, 17)
    return norm_gain(key)


def level_of(rng, extent, cuts, smallest, high):
    def one(position, shards_of):
        steps = jax.random.uniform(jax.random.fold_in(jax.random.fold_in(rng, 6), position), (shards_of,), jnp.float32, smallest / len(cuts), high / len(cuts))
        return jnp.repeat(jnp.exp(steps), extent[position] // shards_of).reshape((-1,) + (1,) * (len(extent) - position - 1))

    level = one(*cuts[0])
    for cut in cuts[1:]:
        level = level * one(*cut)
    return level


def bell_draw(key, shape, deviation, most, cuts=(), kind=jnp.bfloat16):
    drawn = jax.random.normal(key, shape, jnp.float32) * deviation
    if len(cuts) > 0:
        drawn = level_of(key, shape, cuts, -0.22, 0.18) * drawn
    return jnp.clip(drawn, min=-most, max=most).astype(kind)


def setup_inputs(seed: int = 0) -> dict:
    key_list = jax.random.split(jax.random.key(seed), 16)
    hidden_low = bell_draw(key_list[0], (TOKENS_LO, D), 0.3, 2.0, ((0, 16),))
    query_low = draw_query_low(jax.random.fold_in(key_list[15], 71), 0)
    key_low = draw_key_low(jax.random.fold_in(key_list[15], 71), 0)
    value_low = bell_draw(key_list[3], (TOKENS_LO, D), 1.0, 6.0, ((0, 16), (1, 8)))
    out_weight = bell_draw(key_list[4], (D, D), D ** -0.5, 0.09375, ((0, 8),))
    latent_weight = bell_draw(key_list[5], (D, C), D ** -0.5, 0.09375)
    conv_first = bell_draw(key_list[6], (3, 3, 3, C, MID), (27 * C) ** -0.5, 0.109375)
    bias_first = bell_draw(key_list[7], (MID,), 0.5, 3.0, (), jnp.float32)
    conv_second = bell_draw(key_list[8], (MID, 4 * C), MID ** -0.5, 0.25)
    bias_second = bell_draw(key_list[9], (4 * C,), 0.5, 3.0, (), jnp.float32)
    query_weight = draw_query_weight(jax.random.fold_in(key_list[15], 71), 0)
    key_weight = draw_key_weight(jax.random.fold_in(key_list[15], 71), 0)
    value_weight = bell_draw(key_list[12], (C, D), C ** -0.5, 0.5)
    query_gain = draw_query_gain(jax.random.fold_in(key_list[15], 71), 0)
    key_gain = draw_key_gain(jax.random.fold_in(key_list[15], 71), 0)
    return {"hidden_low": hidden_low, "query_low": query_low, "key_low": key_low, "value_low": value_low, "out_weight": out_weight, "latent_weight": latent_weight, "conv_first": conv_first, "bias_first": bias_first, "conv_second": conv_second, "bias_second": bias_second, "query_weight": query_weight, "key_weight": key_weight, "value_weight": value_weight, "query_gain": query_gain, "key_gain": key_gain}


def attention(queries, key_rows, value_rows):
    row_count = queries.shape[0]
    scale = 1.0 / math.sqrt(HD)

    def per_head(head_index):
        offset = (head_index * HD).astype(jnp.int32)
        query_part = lax.dynamic_slice_in_dim(queries, offset, HD, 1)
        key_part = lax.dynamic_slice_in_dim(key_rows, offset, HD, 1)
        value_part = lax.dynamic_slice_in_dim(value_rows, offset, HD, 1)
        scores = jnp.dot(query_part, key_part.T, preferred_element_type=jnp.float32) * scale
        top_score = lax.optimization_barrier(jnp.max(scores, axis=1, keepdims=True))
        expsum = jnp.exp(scores - top_score)
        totals = lax.optimization_barrier(jnp.sum(expsum, axis=1, keepdims=True))
        numerator = jnp.dot(expsum.astype(jnp.bfloat16), value_part, preferred_element_type=jnp.float32)
        return (numerator / totals).astype(jnp.bfloat16)
    heads_out = lax.map(per_head, jnp.arange(HEADS, dtype=jnp.int32))
    return heads_out.transpose(1, 0, 2).reshape(row_count, HEADS * HD)

def upsample_frame(window, frame_low, conv_first, bias_first, conv_second, bias_second):
    rows_low = frame_low.shape[0]
    cols_low = frame_low.shape[1]
    channels = frame_low.shape[2]
    padded = jnp.pad(window, ((0, 0), (1, 1), (1, 1), (0, 0)))
    patches = []
    for frame_off in range(3):
        for row_off in range(3):
            for col_off in range(3):
                patches.append(padded[frame_off, row_off:row_off + rows_low, col_off:col_off + cols_low, :])
    stacked = jnp.concatenate(patches, axis=2).reshape(rows_low * cols_low, 27 * channels)
    kernel = conv_first.reshape(27 * channels, conv_first.shape[4])
    middle = jax.nn.silu(jnp.dot(stacked, kernel, preferred_element_type=jnp.float32) + bias_first).astype(jnp.bfloat16)
    sub_pixels = jnp.dot(middle, conv_second, preferred_element_type=jnp.float32) + bias_second
    sub_pixels = sub_pixels.reshape(rows_low, cols_low, 2, 2, channels).transpose(0, 2, 1, 3, 4)
    sub_pixels = sub_pixels.reshape(2 * rows_low, 2 * cols_low, channels)
    nearest = jnp.repeat(jnp.repeat(frame_low.astype(jnp.float32), 2, axis=0), 2, axis=1)
    return (sub_pixels + nearest).astype(jnp.bfloat16)

def normed(projected, gain):
    return projected * lax.rsqrt(lax.optimization_barrier(jnp.mean(projected * projected, axis=1, keepdims=True)) + 1e-06) * gain

def reference(hidden_low, query_low, key_low, value_low, out_weight, latent_weight, conv_first, bias_first, conv_second, bias_second, query_weight, key_weight, value_weight, query_gain, key_gain):
    attn_low = attention(query_low, key_low, value_low)
    mixture = (hidden_low.astype(jnp.float32) + jnp.dot(attn_low, out_weight, preferred_element_type=jnp.float32)).astype(jnp.bfloat16)
    latent = jnp.dot(mixture, latent_weight, preferred_element_type=jnp.float32).astype(jnp.bfloat16)
    frames_low = latent.reshape(N_SEQ, H_LO, W_LO, C)
    padded_time = jnp.pad(frames_low, ((1, 1), (0, 0), (0, 0), (0, 0)))
    windows = jnp.stack([padded_time[0:N_SEQ], padded_time[1:N_SEQ + 1], padded_time[2:N_SEQ + 2]], axis=1)
    high = jax.vmap(lambda window, frame_low: upsample_frame(window, frame_low, conv_first, bias_first, conv_second, bias_second))(windows, frames_low)
    upsampled = high.reshape(TOKENS_HI, C)
    hi_query = normed(jnp.dot(upsampled, query_weight, preferred_element_type=jnp.float32), query_gain).astype(jnp.bfloat16)
    hi_key = normed(jnp.dot(upsampled, key_weight, preferred_element_type=jnp.float32), key_gain).astype(jnp.bfloat16)
    hi_value = jnp.dot(upsampled, value_weight, preferred_element_type=jnp.float32).astype(jnp.bfloat16)
    hires_attention = attention(hi_query, hi_key, hi_value)
    return (hires_attention, upsampled)
```

```python
import functools
import math

import jax
import jax.numpy as jnp
from jax import lax
from jax.experimental import pallas as pl
from jax.experimental.pallas import tpu as pltpu
from jax.sharding import PartitionSpec as P

HD = 128
H_LO = 4
W_LO = 32
FRAMES = 16
TOK = H_LO * W_LO
KEYS = 4 * FRAMES * TOK
LOG2E = 1.4426950408889634
SCALE = LOG2E / math.sqrt(HD)
BF = jnp.bfloat16
F32 = jnp.float32
NT = (((1,), (1,)), ((), ()))


def dot(a, b):
    return jnp.dot(a, b, preferred_element_type=F32)


def dot_nt(a, b):
    return lax.dot_general(a, b, NT, preferred_element_type=F32)


def split2(x):
    high = x.astype(BF)
    low = (x - high.astype(F32)).astype(BF)
    return jnp.concatenate([high, low], axis=1)


def dot2(a, b2):
    both = dot(a, b2)
    half = both.shape[1] // 2
    return both[:, :half] + both[:, half:]


def whole(shape):
    return pl.BlockSpec(shape, lambda *_: (0,) * len(shape))


def pack_kernel(pos, q_ref, k_ref, v_ref, *outs):
    for shift, out in enumerate(outs):
        head = lax.rem(pos[1] + shift, 4)
        columns = pl.ds(pl.multiple_of(head * HD, HD), HD)
        out[:, 0:HD] = q_ref[:, columns]
        out[:, HD : 2 * HD] = k_ref[:, columns]
        out[:, 2 * HD : 3 * HD] = v_ref[:, columns]


def pack(pos, q, k, v):
    piece = jax.ShapeDtypeStruct((TOK, 3 * HD), BF)
    return pl.pallas_call(
        pack_kernel,
        grid_spec=pltpu.PrefetchScalarGridSpec(
            num_scalar_prefetch=1,
            grid=(1,),
            in_specs=[whole(q.shape)] * 3,
            out_specs=[whole(piece.shape)] * 4,
        ),
        out_shape=[piece] * 4,
        name="pack",
    )(pos, q, k, v)


def prep_kernel(pos, ow, lw, hid, wqh, wkh, gq, gk, wq, wk, w2_out, hl_out, m_out, gq_out, gk_out):
    del pos
    w2_out[...] = split2(dot(ow[...], lw[...]))
    hl_out[...] = dot(hid[...], lw[...])
    gain = gq[...] * gk[...]
    for head in range(4):
        cols = slice(head * HD, (head + 1) * HD)
        left = split2(wqh[:, cols].astype(F32) * gain[:, cols])
        right = wkh[:, cols]
        m_out[head] = split2(dot_nt(left[:, :HD], right) + dot_nt(left[:, HD:], right))
    gq_out[...] = split2(dot_nt(wq[...], wq[...]))
    gk_out[...] = split2(dot_nt(wk[...], wk[...]))


def prep(pos, out_weight, latent_weight, hidden, query_weight, key_weight, query_gain, key_gain):
    width = hidden.shape[1]
    share = TOK // 8
    group = 4 * HD
    return pl.pallas_call(
        prep_kernel,
        grid_spec=pltpu.PrefetchScalarGridSpec(
            num_scalar_prefetch=1,
            grid=(1,),
            in_specs=[
                pl.BlockSpec((HD, width), lambda i, pos: (pos[1], 0)),
                whole(latent_weight.shape),
                pl.BlockSpec((share, width), lambda i, pos: (pos[3], 0)),
                pl.BlockSpec((HD, group), lambda i, pos: (0, pos[3])),
                pl.BlockSpec((HD, group), lambda i, pos: (0, pos[3])),
                pl.BlockSpec((1, group), lambda i, pos: (0, pos[3])),
                pl.BlockSpec((1, group), lambda i, pos: (0, pos[3])),
                whole(query_weight.shape),
                whole(key_weight.shape),
            ],
            out_specs=[
                whole((HD, 2 * HD)),
                whole((share, HD)),
                whole((4, HD, 2 * HD)),
                whole((HD, 2 * HD)),
                whole((HD, 2 * HD)),
            ],
        ),
        out_shape=[
            jax.ShapeDtypeStruct((HD, 2 * HD), BF),
            jax.ShapeDtypeStruct((share, HD), F32),
            jax.ShapeDtypeStruct((4, HD, 2 * HD), BF),
            jax.ShapeDtypeStruct((HD, 2 * HD), BF),
            jax.ShapeDtypeStruct((HD, 2 * HD), BF),
        ],
        compiler_params=pltpu.CompilerParams(vmem_limit_bytes=24 * 2**20),
        cost_estimate=pl.CostEstimate(flops=900_000_000, bytes_accessed=5_000_000, transcendentals=0),
        name="prep",
    )(
        pos,
        out_weight,
        latent_weight,
        hidden,
        query_weight,
        key_weight,
        query_gain.reshape(1, -1),
        key_gain.reshape(1, -1),
        query_weight,
        key_weight,
    )


def low_kernel(pos, p0, p1, p2, p3, kv0, kv1, kv2, kv3, w2, hl, out, q_s, part_s):
    z = pos[1]
    for shift, piece in enumerate((p0, p1, p2, p3)):
        q_s[lax.rem(z + 4 - shift, 4)] = piece[:, 0:HD]
    for half in range(2):
        q = q_s[2 * half : 2 * half + 2].reshape(2 * TOK, HD)
        blocks = (kv0, kv1, kv2, kv3)
        scores = [dot_nt(q, kv[:, 0:HD]) * SCALE for kv in blocks]
        top = functools.reduce(jnp.maximum, [jnp.max(s, axis=1, keepdims=True) for s in scores])
        total = jnp.zeros((2 * TOK, 1), F32)
        numerator = jnp.zeros((2 * TOK, HD), F32)
        for s, kv in zip(scores, blocks):
            e = jnp.exp2(s - top)
            total = total + jnp.sum(e, axis=1, keepdims=True)
            numerator = numerator + dot(e.astype(BF), kv[:, HD : 2 * HD])
        attn = (numerator / total).astype(BF)
        part_s[2 * half * TOK : (2 * half + 2) * TOK, :] = dot2(attn, w2[...])
    share = TOK // 8
    rows = pl.ds(pl.multiple_of(z * TOK + pos[3] * share, share), share)
    part_s[rows, :] = part_s[rows, :] + hl[...]
    out[...] = part_s[...].astype(BF)


def low_attention(pos, pieces, kvs, w2, hl):
    args = (*pieces, *kvs, w2, hl)
    return pl.pallas_call(
        low_kernel,
        grid_spec=pltpu.PrefetchScalarGridSpec(
            num_scalar_prefetch=1,
            grid=(1,),
            in_specs=[whole(a.shape) for a in args],
            out_specs=whole((4 * TOK, HD)),
            scratch_shapes=[pltpu.VMEM((4, TOK, HD), BF), pltpu.VMEM((4 * TOK, HD), F32)],
        ),
        out_shape=jax.ShapeDtypeStruct((4 * TOK, HD), BF),
        compiler_params=pltpu.CompilerParams(vmem_limit_bytes=32 * 2**20),
        name="low",
    )(pos, *args)


CHUNK = 4
BLOCK = 2048
TINY = 2.0**-90


def hi_kernel(
    pos,
    lat0,
    lat1,
    lat2,
    lat3,
    conv,
    b1,
    second,
    b2,
    gq,
    gk,
    m,
    wv,
    attn_out,
    up_out,
    grid_s,
    lat_s,
    key_s,
    val_s,
    q_s,
    nat_s,
    acc_s,
    max_s,
):
    x, z, c, g = pos[0], pos[1], pos[2], pos[3]
    for dx, dc, piece in ((0, 0, lat0), (0, 1, lat1), (1, 0, lat2), (1, 1, lat3)):
        px = lax.bitwise_xor(x, dx)
        pc = lax.bitwise_xor(c, dc)
        for pz in range(4):
            lat_s[px * 8 + pz * 2 + pc] = piece[pz * TOK : (pz + 1) * TOK, :]
    grid_s[...] = jnp.zeros_like(grid_s)
    lat = lat_s[...].reshape(FRAMES * TOK, HD).astype(F32)
    column = lax.rem(lax.broadcasted_iota(jnp.int32, (FRAMES * TOK, HD), 0), W_LO)
    left = jnp.where(column == 0, 0.0, pltpu.roll(lat, 1, 0))
    right = jnp.where(column == W_LO - 1, 0.0, pltpu.roll(lat, FRAMES * TOK - 1, 0))
    for index, shifted in enumerate((left, lat, right)):
        grid_s[index, 1 : FRAMES + 1, 1 : H_LO + 1] = shifted.astype(BF).reshape(FRAMES, H_LO, W_LO, HD)

    val_s[:, HD : 2 * HD] = jnp.ones((KEYS, HD), BF)
    biggest = jnp.zeros((1, 1), F32)
    rows = CHUNK * TOK
    for first in range(0, FRAMES, CHUNK):
        taps = []
        for a in range(3):
            for b in range(3):
                for t in range(3):
                    taps.append(grid_s[t, first + a : first + a + CHUNK, b : b + H_LO].reshape(rows, HD))
        middle = dot(jnp.concatenate(taps, axis=1), conv[...]) + b1[...]
        middle = (middle / (1.0 + jnp.exp(-middle))).astype(BF)
        sub = dot(middle, second[...]) + b2[...]
        base = lat_s[first : first + CHUNK].reshape(rows, HD).astype(F32)
        for s in range(4):
            up = (sub[:, s * HD : (s + 1) * HD] + base).astype(BF)
            upf = up.astype(F32)
            square = jnp.sum(dot2(up, gk[...]) * upf, axis=1, keepdims=True)
            inverse = lax.rsqrt(jnp.maximum(square, 0.0) * (1.0 / 4096.0) + 1e-6)
            key = (upf * inverse).astype(BF)
            where = pl.ds(s * FRAMES * TOK + first * TOK, rows)
            val_s[where, 0:HD] = up
            key_s[where, :] = key
            keyf = key.astype(F32)
            length = jnp.sum(keyf * keyf, axis=1, keepdims=True)
            biggest = jnp.maximum(biggest, jnp.max(length, axis=0, keepdims=True))

    frame = x * 8 + z * 2 + c
    own = jnp.concatenate(
        [val_s[pl.ds(pl.multiple_of(s * FRAMES * TOK + frame * TOK, TOK), TOK), 0:HD] for s in range(4)], axis=0
    )
    to = lax.broadcasted_iota(jnp.int32, (4 * TOK, 4 * TOK), 0)
    source = lax.broadcasted_iota(jnp.int32, (4 * TOK, 4 * TOK), 1)
    row, col = to // (2 * W_LO), lax.rem(to, 2 * W_LO)
    wanted = (lax.rem(row, 2) * 2 + lax.rem(col, 2)) * TOK + (row // 2) * W_LO + col // 2
    natural = dot(jnp.where(source == wanted, 1.0, 0.0).astype(BF), own)
    nat_s[...] = natural
    up_out[...] = nat_s[pl.ds(pl.multiple_of(g * 2 * W_LO, 2 * W_LO), 2 * W_LO), :].astype(BF)
    mine = natural.astype(BF)
    square = jnp.sum(dot2(mine, gq[...]) * natural, axis=1, keepdims=True)
    inverse = lax.rsqrt(jnp.maximum(square, 0.0) * (1.0 / 4096.0) + 1e-6) * SCALE
    for head in range(4):
        q_s[head] = (dot2(mine, m[head]) * inverse).astype(BF)

    def one_head(head, carry):
        q = q_s[head]
        qf = q.astype(F32)
        bound = jnp.sqrt(jnp.sum(qf * qf, axis=1, keepdims=True) * biggest)

        def step(j, acc):
            keys = pl.ds(pl.multiple_of(j * BLOCK, BLOCK), BLOCK)
            scores = dot_nt(q, key_s[keys, :])
            return acc + dot(jnp.exp2(scores - bound).astype(BF), val_s[keys, :])

        acc = lax.fori_loop(0, KEYS // BLOCK, step, jnp.zeros((4 * TOK, 2 * HD), F32), unroll=2)
        acc_s[...] = acc
        weakest = jnp.min(acc[:, HD:])

        @pl.when(jnp.logical_not(weakest > TINY))
        def _():
            acc_s[...] = jnp.zeros_like(acc_s)
            max_s[...] = jnp.full_like(max_s, -1e30)

            def careful(j, carry):
                keys = pl.ds(pl.multiple_of(j * 512, 512), 512)
                scores = dot_nt(q_s[head], key_s[keys, :])
                before = max_s[:, 0:1]
                top = jnp.maximum(before, jnp.max(scores, axis=1, keepdims=True))
                weights = jnp.exp2(scores - top).astype(BF)
                acc_s[...] = acc_s[...] * jnp.exp2(before - top) + dot(weights, val_s[keys, :])
                max_s[...] = jnp.broadcast_to(top, max_s.shape)
                return carry

            lax.fori_loop(0, KEYS // 512, careful, 0)

        mixed = (acc_s[:, :HD] / acc_s[:, HD:]).astype(BF)
        columns = pl.ds(pl.multiple_of(head * HD, HD), HD)
        attn_out[:, columns] = dot(mixed, wv[:, columns]).astype(BF)
        return carry

    lax.fori_loop(0, 4, one_head, 0)


def hi_attention(pos, lats, conv_first, bias_first, conv_second, bias_second, gq, gk, m, value_weight):
    mid = conv_second.shape[0]
    conv = conv_first.reshape(27 * HD, mid)
    args = (*lats, conv, bias_first.reshape(1, -1), conv_second, bias_second.reshape(1, -1), gq, gk, m, value_weight)
    in_specs = [whole(a.shape) for a in args]
    in_specs[-1] = pl.BlockSpec((HD, 4 * HD), lambda i, pos: (0, pos[3]))
    return pl.pallas_call(
        hi_kernel,
        grid_spec=pltpu.PrefetchScalarGridSpec(
            num_scalar_prefetch=1,
            grid=(1,),
            in_specs=in_specs,
            out_specs=[whole((4 * TOK, 4 * HD)), whole((2 * W_LO, HD))],
            scratch_shapes=[
                pltpu.VMEM((3, FRAMES + 2, H_LO + 2, W_LO, HD), BF),
                pltpu.VMEM((FRAMES, TOK, HD), BF),
                pltpu.VMEM((KEYS, HD), BF),
                pltpu.VMEM((KEYS, 2 * HD), BF),
                pltpu.VMEM((4, 4 * TOK, HD), BF),
                pltpu.VMEM((4 * TOK, HD), F32),
                pltpu.VMEM((4 * TOK, 2 * HD), F32),
                pltpu.VMEM((4 * TOK, HD), F32),
            ],
        ),
        out_shape=[
            jax.ShapeDtypeStruct((4 * TOK, 4 * HD), BF),
            jax.ShapeDtypeStruct((2 * W_LO, HD), BF),
        ],
        compiler_params=pltpu.CompilerParams(vmem_limit_bytes=56 * 2**20),
        name="hi",
    )(pos, *args)


def swap(axis, bit):
    return [(i, i ^ bit) for i in range(16 if axis == "seq" else 8)]


def z_shift(step):
    return [(i, (i & 9) | ((((i >> 1) + step) & 3) << 1)) for i in range(16)]


CORE, X_HI = ("seq", 1), ("seq", 8)


def send(value, link):
    axis, bit = link
    return lax.ppermute(value, axis, swap(axis, bit))


def local(
    hidden_low,
    query_low,
    key_low,
    value_low,
    out_weight,
    latent_weight,
    conv_first,
    bias_first,
    conv_second,
    bias_second,
    query_weight,
    key_weight,
    value_weight,
    query_gain,
    key_gain,
):
    seq, head = lax.axis_index("seq"), lax.axis_index("head")
    pos = jnp.stack([seq // 8, (seq // 2) % 4, seq % 2, head]).astype(jnp.int32)
    pieces = pack(pos, query_low, key_low, value_low)
    pieces = [pieces[0]] + [
        lax.ppermute(pieces[step], "seq", z_shift(step)) for step in (1, 2, 3)
    ]
    w2, hl, m, gq, gk = prep(
        pos, out_weight, latent_weight, hidden_low, query_weight, key_weight, query_gain, key_gain
    )
    kv = jnp.concatenate([piece[:, HD:] for piece in pieces], axis=0)
    kv_x = send(kv, X_HI)
    kv_c = send(kv, CORE)
    kv_xc = send(kv_x, CORE)
    latent = low_attention(pos, pieces, (kv, kv_c, kv_x, kv_xc), w2, hl)
    for link in (("head", 1), ("head", 2), ("head", 4), ("seq", 2), ("seq", 4)):
        latent = (latent.astype(F32) + send(latent, link).astype(F32)).astype(BF)
    lat_x = send(latent, X_HI)
    lat_c = send(latent, CORE)
    lat_xc = send(lat_x, CORE)
    attn, up = hi_attention(
        pos,
        (latent, lat_c, lat_x, lat_xc),
        conv_first,
        bias_first,
        conv_second,
        bias_second,
        gq,
        gk,
        m,
        value_weight,
    )
    return attn, up


def solution(mesh):
    placed = (
        P("seq", None),
        P("seq", "head"),
        P("seq", "head"),
        P("seq", "head"),
        P("head", None),
    ) + (P(),) * 10
    return jax.shard_map(
        local,
        mesh=mesh,
        in_specs=placed,
        out_specs=(P("seq", "head"), P(("seq", "head"), None)),
        check_vma=False,
    )
```

```python
import functools
import math

import jax
import jax.numpy as jnp
from jax import lax
from jax.experimental import pallas as pl
from jax.experimental.pallas import tpu as pltpu
from jax.sharding import PartitionSpec as P

HD = 128
H_LO = 4
W_LO = 32
FRAMES = 16
TOK = H_LO * W_LO
KEYS = 4 * FRAMES * TOK
LOG2E = 1.4426950408889634
SCALE = LOG2E / math.sqrt(HD)
BF = jnp.bfloat16
F32 = jnp.float32
VMEM = 60 * 2**20
NT = (((1,), (1,)), ((), ()))


def dot(a, b):
    return jnp.dot(a, b, preferred_element_type=F32)


def dot_nt(a, b):
    return lax.dot_general(a, b, NT, preferred_element_type=F32)


def split2(x):
    high = x.astype(BF)
    low = (x - high.astype(F32)).astype(BF)
    return jnp.concatenate([high, low], axis=1)


def dot2(a, b2):
    both = dot(a, b2)
    half = both.shape[1] // 2
    return both[:, :half] + both[:, half:]


def whole(shape):
    return pl.BlockSpec(shape, lambda *_: (0,) * len(shape))


def pack_kernel(pos, q_ref, k_ref, v_ref, o0, o1, o2, o3, sems):
    copies = []
    for shift, out in enumerate((o0, o1, o2, o3)):
        head = lax.rem(pos[1] + shift, 4)
        columns = pl.ds(pl.multiple_of(head * HD, HD), HD)
        for part, ref in enumerate((q_ref, k_ref, v_ref)):
            copies.append(
                pltpu.make_async_copy(
                    ref.at[:, columns], out.at[:, part * HD : (part + 1) * HD], sems.at[shift, part]
                )
            )
    for copy in copies:
        copy.start()
    for copy in copies:
        copy.wait()


def pack(pos, q, k, v):
    piece = jax.ShapeDtypeStruct((TOK, 3 * HD), BF)
    anywhere = pl.BlockSpec(memory_space=pl.ANY)
    return pl.pallas_call(
        pack_kernel,
        grid_spec=pltpu.PrefetchScalarGridSpec(
            num_scalar_prefetch=1,
            grid=(1,),
            in_specs=[anywhere] * 3,
            out_specs=[anywhere] * 4,
            scratch_shapes=[pltpu.SemaphoreType.DMA((4, 3))],
        ),
        out_shape=[piece] * 4,
        compiler_params=pltpu.CompilerParams(vmem_limit_bytes=VMEM),
        name="pack",
    )(pos, q, k, v)


def prep_kernel(pos, ow, lw, hid, wqh, wkh, gq, gk, wq, wk, w2_out, hl_out, m_out, gq_out, gk_out):
    del pos
    w2_out[...] = split2(dot(ow[...], lw[...]))
    hl_out[...] = dot(hid[...], lw[...])
    gain = gq[...] * gk[...]
    for head in range(4):
        cols = slice(head * HD, (head + 1) * HD)
        left = split2(wqh[:, cols].astype(F32) * gain[:, cols])
        right = wkh[:, cols]
        m_out[head] = split2(dot_nt(left[:, :HD], right) + dot_nt(left[:, HD:], right))
    gq_out[...] = split2(dot_nt(wq[...], wq[...]))
    gk_out[...] = split2(dot_nt(wk[...], wk[...]))


def prep(pos, out_weight, latent_weight, hidden, query_weight, key_weight, query_gain, key_gain):
    width = hidden.shape[1]
    share = TOK // 8
    group = 4 * HD
    return pl.pallas_call(
        prep_kernel,
        grid_spec=pltpu.PrefetchScalarGridSpec(
            num_scalar_prefetch=1,
            grid=(1,),
            in_specs=[
                pl.BlockSpec((HD, width), lambda i, pos: (pos[1], 0)),
                whole(latent_weight.shape),
                pl.BlockSpec((share, width), lambda i, pos: (pos[3], 0)),
                pl.BlockSpec((HD, group), lambda i, pos: (0, pos[3])),
                pl.BlockSpec((HD, group), lambda i, pos: (0, pos[3])),
                pl.BlockSpec((1, group), lambda i, pos: (0, pos[3])),
                pl.BlockSpec((1, group), lambda i, pos: (0, pos[3])),
                whole(query_weight.shape),
                whole(key_weight.shape),
            ],
            out_specs=[
                whole((HD, 2 * HD)),
                whole((share, HD)),
                whole((4, HD, 2 * HD)),
                whole((HD, 2 * HD)),
                whole((HD, 2 * HD)),
            ],
        ),
        out_shape=[
            jax.ShapeDtypeStruct((HD, 2 * HD), BF),
            jax.ShapeDtypeStruct((share, HD), F32),
            jax.ShapeDtypeStruct((4, HD, 2 * HD), BF),
            jax.ShapeDtypeStruct((HD, 2 * HD), BF),
            jax.ShapeDtypeStruct((HD, 2 * HD), BF),
        ],
        compiler_params=pltpu.CompilerParams(vmem_limit_bytes=VMEM),
        cost_estimate=pl.CostEstimate(flops=900_000_000, bytes_accessed=5_000_000, transcendentals=0),
        name="prep",
    )(
        pos,
        out_weight,
        latent_weight,
        hidden,
        query_weight,
        key_weight,
        query_gain.reshape(1, -1),
        key_gain.reshape(1, -1),
        query_weight,
        key_weight,
    )


def low_kernel(pos, p0, p1, p2, p3, kv0, kv1, kv2, kv3, w2, hl, out, q_s, part_s):
    z = pos[1]
    for shift, piece in enumerate((p0, p1, p2, p3)):
        q_s[lax.rem(z + 4 - shift, 4)] = piece[:, 0:HD]
    for half in range(2):
        q = q_s[2 * half : 2 * half + 2].reshape(2 * TOK, HD)
        blocks = (kv0, kv1, kv2, kv3)
        scores = [dot_nt(q, kv[:, 0:HD]) * SCALE for kv in blocks]
        top = functools.reduce(jnp.maximum, [jnp.max(s, axis=1, keepdims=True) for s in scores])
        total = jnp.zeros((2 * TOK, 1), F32)
        numerator = jnp.zeros((2 * TOK, HD), F32)
        for s, kv in zip(scores, blocks):
            e = jnp.exp2(s - top)
            total = total + jnp.sum(e, axis=1, keepdims=True)
            numerator = numerator + dot(e.astype(BF), kv[:, HD : 2 * HD])
        attn = (numerator / total).astype(BF)
        part_s[2 * half * TOK : (2 * half + 2) * TOK, :] = dot2(attn, w2[...])
    share = TOK // 8
    rows = pl.ds(pl.multiple_of(z * TOK + pos[3] * share, share), share)
    part_s[rows, :] = part_s[rows, :] + hl[...]
    out[...] = part_s[...].astype(BF)


def low_attention(pos, pieces, kvs, w2, hl):
    args = (*pieces, *kvs, w2, hl)
    return pl.pallas_call(
        low_kernel,
        grid_spec=pltpu.PrefetchScalarGridSpec(
            num_scalar_prefetch=1,
            grid=(1,),
            in_specs=[whole(a.shape) for a in args],
            out_specs=whole((4 * TOK, HD)),
            scratch_shapes=[pltpu.VMEM((4, TOK, HD), BF), pltpu.VMEM((4 * TOK, HD), F32)],
        ),
        out_shape=jax.ShapeDtypeStruct((4 * TOK, HD), BF),
        compiler_params=pltpu.CompilerParams(vmem_limit_bytes=VMEM),
        name="low",
    )(pos, *args)


CHUNK = 4
BLOCK = 2048
TINY = 2.0**-90


def hi_kernel(
    pos,
    lat0,
    lat1,
    lat2,
    lat3,
    conv,
    b1,
    second,
    b2,
    gq,
    gk,
    m,
    wv,
    attn_out,
    up_out,
    grid_s,
    lat_s,
    key_s,
    val_s,
    q_s,
    nat_s,
    acc_s,
    bound_s,
):
    x, z, c, g = pos[0], pos[1], pos[2], pos[3]
    for dx, dc, piece in ((0, 0, lat0), (0, 1, lat1), (1, 0, lat2), (1, 1, lat3)):
        px = lax.bitwise_xor(x, dx)
        pc = lax.bitwise_xor(c, dc)
        for pz in range(4):
            lat_s[px * 8 + pz * 2 + pc] = piece[pz * TOK : (pz + 1) * TOK, :]
    grid_s[...] = jnp.zeros_like(grid_s)
    lat = lat_s[...].reshape(FRAMES * TOK, HD).astype(F32)
    column = lax.rem(lax.broadcasted_iota(jnp.int32, (FRAMES * TOK, HD), 0), W_LO)
    left = jnp.where(column == 0, 0.0, pltpu.roll(lat, 1, 0))
    right = jnp.where(column == W_LO - 1, 0.0, pltpu.roll(lat, FRAMES * TOK - 1, 0))
    for index, shifted in enumerate((left, lat, right)):
        grid_s[index, 1 : FRAMES + 1, 1 : H_LO + 1] = shifted.astype(BF).reshape(FRAMES, H_LO, W_LO, HD)

    val_s[:, HD : 2 * HD] = jnp.ones((KEYS, HD), BF)
    biggest = jnp.zeros((1, 1), F32)
    rows = CHUNK * TOK
    for first in range(0, FRAMES, CHUNK):
        taps = []
        for a in range(3):
            for b in range(3):
                for t in range(3):
                    taps.append(grid_s[t, first + a : first + a + CHUNK, b : b + H_LO].reshape(rows, HD))
        middle = dot(jnp.concatenate(taps, axis=1), conv[...]) + b1[...]
        middle = (middle * (0.5 * jnp.tanh(0.5 * middle) + 0.5)).astype(BF)
        sub = dot(middle, second[...]) + b2[...]
        base = lat_s[first : first + CHUNK].reshape(rows, HD).astype(F32)
        for s in range(4):
            up = (sub[:, s * HD : (s + 1) * HD] + base).astype(BF)
            upf = up.astype(F32)
            square = jnp.sum(dot2(up, gk[...]) * upf, axis=1, keepdims=True)
            inverse = lax.rsqrt(jnp.maximum(square, 0.0) * (1.0 / 4096.0) + 1e-6)
            key = (upf * inverse).astype(BF)
            where = pl.ds(s * FRAMES * TOK + first * TOK, rows)
            val_s[where, 0:HD] = up
            key_s[where, :] = key
            keyf = key.astype(F32)
            length = jnp.sum(keyf * keyf, axis=1, keepdims=True)
            biggest = jnp.maximum(biggest, jnp.max(length, axis=0, keepdims=True))

    frame = x * 8 + z * 2 + c
    own = jnp.concatenate(
        [val_s[pl.ds(pl.multiple_of(s * FRAMES * TOK + frame * TOK, TOK), TOK), 0:HD] for s in range(4)], axis=0
    )
    to = lax.broadcasted_iota(jnp.int32, (4 * TOK, 4 * TOK), 0)
    source = lax.broadcasted_iota(jnp.int32, (4 * TOK, 4 * TOK), 1)
    p, r = (to >> 6) & 1, to & 1
    wanted = (((p << 1) | r) << 7) | ((to >> 7) << 5) | ((to >> 1) & (W_LO - 1))
    natural = dot(jnp.where(source == wanted, 1.0, 0.0).astype(BF), own)
    nat_s[...] = natural
    up_out[...] = nat_s[pl.ds(pl.multiple_of(g * 2 * W_LO, 2 * W_LO), 2 * W_LO), :].astype(BF)
    mine = natural.astype(BF)
    square = jnp.sum(dot2(mine, gq[...]) * natural, axis=1, keepdims=True)
    inverse = lax.rsqrt(jnp.maximum(square, 0.0) * (1.0 / 4096.0) + 1e-6) * SCALE
    for head in range(4):
        q_s[head] = (dot2(mine, m[head]) * inverse).astype(BF)

    for head in range(4):
        qf = q_s[head].astype(F32)
        bound = jnp.sqrt(jnp.sum(qf * qf, axis=1, keepdims=True) * biggest)
        bound_s[head] = jnp.broadcast_to(bound, (4 * TOK, HD))
    acc_s[...] = jnp.zeros_like(acc_s)

    def step(j, carry):
        keys = pl.ds(pl.multiple_of(j * BLOCK, BLOCK), BLOCK)
        for head in range(4):
            scores = dot_nt(q_s[head], key_s[keys, :])
            weights = jnp.exp2(scores - bound_s[head, :, 0:1]).astype(BF)
            acc_s[head] += dot(weights, val_s[keys, :])
        return carry

    lax.fori_loop(0, KEYS // BLOCK, step, 0)

    @pl.when(jnp.logical_not(jnp.min(acc_s[:, :, HD:]) > TINY))
    def _():
        def careful_head(head, carry):
            acc_s[head] = jnp.zeros((4 * TOK, 2 * HD), F32)
            bound_s[head] = jnp.full((4 * TOK, HD), -1e30, F32)

            def careful(j, carry):
                keys = pl.ds(pl.multiple_of(j * 512, 512), 512)
                scores = dot_nt(q_s[head], key_s[keys, :])
                before = bound_s[head, :, 0:1]
                top = jnp.maximum(before, jnp.max(scores, axis=1, keepdims=True))
                weights = jnp.exp2(scores - top).astype(BF)
                acc_s[head] = acc_s[head] * jnp.exp2(before - top) + dot(weights, val_s[keys, :])
                bound_s[head] = jnp.broadcast_to(top, (4 * TOK, HD))
                return carry

            return lax.fori_loop(0, KEYS // 512, careful, carry)

        lax.fori_loop(0, 4, careful_head, 0)

    for head in range(4):
        mixed = (acc_s[head, :, :HD] / acc_s[head, :, HD:]).astype(BF)
        columns = slice(head * HD, (head + 1) * HD)
        attn_out[:, columns] = dot(mixed, wv[:, columns]).astype(BF)


def hi_attention(pos, lats, conv_first, bias_first, conv_second, bias_second, gq, gk, m, value_weight):
    mid = conv_second.shape[0]
    conv = conv_first.reshape(27 * HD, mid)
    args = (*lats, conv, bias_first.reshape(1, -1), conv_second, bias_second.reshape(1, -1), gq, gk, m, value_weight)
    in_specs = [whole(a.shape) for a in args]
    in_specs[-1] = pl.BlockSpec((HD, 4 * HD), lambda i, pos: (0, pos[3]))
    return pl.pallas_call(
        hi_kernel,
        grid_spec=pltpu.PrefetchScalarGridSpec(
            num_scalar_prefetch=1,
            grid=(1,),
            in_specs=in_specs,
            out_specs=[whole((4 * TOK, 4 * HD)), whole((2 * W_LO, HD))],
            scratch_shapes=[
                pltpu.VMEM((3, FRAMES + 2, H_LO + 2, W_LO, HD), BF),
                pltpu.VMEM((FRAMES, TOK, HD), BF),
                pltpu.VMEM((KEYS, HD), BF),
                pltpu.VMEM((KEYS, 2 * HD), BF),
                pltpu.VMEM((4, 4 * TOK, HD), BF),
                pltpu.VMEM((4 * TOK, HD), F32),
                pltpu.VMEM((4, 4 * TOK, 2 * HD), F32),
                pltpu.VMEM((4, 4 * TOK, HD), F32),
            ],
        ),
        out_shape=[
            jax.ShapeDtypeStruct((4 * TOK, 4 * HD), BF),
            jax.ShapeDtypeStruct((2 * W_LO, HD), BF),
        ],
        compiler_params=pltpu.CompilerParams(vmem_limit_bytes=VMEM),
        name="hi",
    )(pos, *args)


def z_shift(step):
    return [(i, (i & 9) | ((((i >> 1) + step) & 3) << 1)) for i in range(16)]


def trade(value, partner):
    pairs = []
    for seq in range(16):
        for head in range(8):
            x, y, z, core = (seq >> 3) * 2 + (head & 1), head >> 1, (seq >> 1) & 3, seq & 1
            x, y, z, core = partner(x, y, z, core)
            other = ((x >> 1) * 8 + z * 2 + core) * 8 + y * 2 + (x & 1)
            pairs.append((seq * 8 + head, other))
    return lax.ppermute(value, ("seq", "head"), pairs)


def to_core(x, y, z, core):
    return x, y, z, core ^ 1


def to_x_far(x, y, z, core):
    return x ^ 2, y, z, core


def to_x_near(x, y, z, core):
    return x ^ 3, y, z, core


HOPS = (("x", 1), ("y", 1), ("y", 3), ("z", 1), ("z", 3))


def sum_step(step):
    def partner(x, y, z, core):
        axis, bit = HOPS[(step + core) % 5]
        if axis == "x":
            return x ^ bit, y, z, core
        if axis == "y":
            return x, y ^ bit, z, core
        return x, y, z ^ bit, core

    return partner


def local(
    hidden_low,
    query_low,
    key_low,
    value_low,
    out_weight,
    latent_weight,
    conv_first,
    bias_first,
    conv_second,
    bias_second,
    query_weight,
    key_weight,
    value_weight,
    query_gain,
    key_gain,
):
    seq, head = lax.axis_index("seq"), lax.axis_index("head")
    pos = jnp.stack([seq // 8, (seq // 2) % 4, seq % 2, head]).astype(jnp.int32)
    pieces = pack(pos, query_low, key_low, value_low)
    pieces = [pieces[0]] + [
        lax.ppermute(pieces[step], "seq", z_shift(step)) for step in (1, 2, 3)
    ]
    w2, hl, m, gq, gk = prep(
        pos, out_weight, latent_weight, hidden_low, query_weight, key_weight, query_gain, key_gain
    )
    kv = jnp.concatenate([piece[:, HD:] for piece in pieces], axis=0)
    kv_x = trade(kv, to_x_far)
    kv_c = trade(kv, to_core)
    kv_xc = trade(kv_x, to_core)
    latent = low_attention(pos, pieces, (kv, kv_c, kv_x, kv_xc), w2, hl)
    for step in range(5):
        latent = (latent.astype(F32) + trade(latent, sum_step(step)).astype(F32)).astype(BF)
    lat_x = trade(latent, to_x_near)
    lat_c = trade(latent, to_core)
    lat_xc = trade(lat_x, to_core)
    attn, up = hi_attention(
        pos,
        (latent, lat_c, lat_x, lat_xc),
        conv_first,
        bias_first,
        conv_second,
        bias_second,
        gq,
        gk,
        m,
        value_weight,
    )
    return attn, up


def solution(mesh):
    placed = (
        P("seq", None),
        P("seq", "head"),
        P("seq", "head"),
        P("seq", "head"),
        P("head", None),
    ) + (P(),) * 10
    return jax.shard_map(
        local,
        mesh=mesh,
        in_specs=placed,
        out_specs=(P("seq", "head"), P(("seq", "head"), None)),
        check_vma=False,
    )
```

```python
import functools
import math

import jax
import jax.numpy as jnp
from jax import lax
from jax.experimental import pallas as pl
from jax.experimental.pallas import tpu as pltpu
from jax.sharding import PartitionSpec as P

HD = 128
H_LO = 4
W_LO = 32
FRAMES = 16
TOK = H_LO * W_LO
KEYS = 4 * FRAMES * TOK
LOG2E = 1.4426950408889634
SCALE = LOG2E / math.sqrt(HD)
BF = jnp.bfloat16
F32 = jnp.float32
SMALL, LARGE = 16 * 2**20, 46 * 2**20
NT = (((1,), (1,)), ((), ()))


def dot(a, b):
    return jnp.dot(a, b, preferred_element_type=F32)


def dot_nt(a, b):
    return lax.dot_general(a, b, NT, preferred_element_type=F32)


def split2(x):
    high = x.astype(BF)
    low = (x - high.astype(F32)).astype(BF)
    return jnp.concatenate([high, low], axis=1)


def dot2(a, b2):
    both = dot(a, b2)
    half = both.shape[1] // 2
    return both[:, :half] + both[:, half:]


def whole(shape):
    return pl.BlockSpec(shape, lambda *_: (0,) * len(shape))


def pack_kernel(pos, q_ref, k_ref, v_ref, *outs):
    for shift, out in enumerate(outs):
        head = lax.rem(pos[1] + shift, 4)
        columns = pl.ds(pl.multiple_of(head * HD, HD), HD)
        out[:, 0:HD] = q_ref[:, columns]
        out[:, HD : 2 * HD] = k_ref[:, columns]
        out[:, 2 * HD : 3 * HD] = v_ref[:, columns]


def pack(pos, q, k, v):
    piece = pltpu.VMEM((TOK, 3 * HD), BF)
    return pl.pallas_call(
        pack_kernel,
        grid_spec=pltpu.PrefetchScalarGridSpec(
            num_scalar_prefetch=1,
            grid=(1,),
            in_specs=[whole(q.shape)] * 3,
            out_specs=[whole(piece.shape)] * 4,
        ),
        out_shape=[piece] * 4,
        compiler_params=pltpu.CompilerParams(vmem_limit_bytes=SMALL),
        name="pack",
    )(pos, *(pltpu.with_memory_space_constraint(array, pltpu.HBM) for array in (q, k, v)))


def prep_kernel(pos, ow, lw, hid, wqh, wkh, gq, gk, wq, wk, w2_out, hl_out, m_out, gq_out, gk_out):
    del pos
    w2_out[...] = split2(dot(ow[...], lw[...]))
    hl_out[...] = dot(hid[...], lw[...])
    gain = gq[...] * gk[...]
    for head in range(4):
        cols = slice(head * HD, (head + 1) * HD)
        left = split2(wqh[:, cols].astype(F32) * gain[:, cols])
        right = wkh[:, cols]
        m_out[head] = split2(dot_nt(left[:, :HD], right) + dot_nt(left[:, HD:], right))
    gq_out[...] = split2(dot_nt(wq[...], wq[...]))
    gk_out[...] = split2(dot_nt(wk[...], wk[...]))


def prep(pos, out_weight, latent_weight, hidden, query_weight, key_weight, query_gain, key_gain):
    width = hidden.shape[1]
    share = TOK // 8
    group = 4 * HD
    return pl.pallas_call(
        prep_kernel,
        grid_spec=pltpu.PrefetchScalarGridSpec(
            num_scalar_prefetch=1,
            grid=(1,),
            in_specs=[
                pl.BlockSpec((HD, width), lambda i, pos: (pos[1], 0)),
                whole(latent_weight.shape),
                pl.BlockSpec((share, width), lambda i, pos: (pos[3], 0)),
                pl.BlockSpec((HD, group), lambda i, pos: (0, pos[3])),
                pl.BlockSpec((HD, group), lambda i, pos: (0, pos[3])),
                pl.BlockSpec((1, group), lambda i, pos: (0, pos[3])),
                pl.BlockSpec((1, group), lambda i, pos: (0, pos[3])),
                whole(query_weight.shape),
                whole(key_weight.shape),
            ],
            out_specs=[
                whole((HD, 2 * HD)),
                whole((share, HD)),
                whole((4, HD, 2 * HD)),
                whole((HD, 2 * HD)),
                whole((HD, 2 * HD)),
            ],
        ),
        out_shape=[
            jax.ShapeDtypeStruct((HD, 2 * HD), BF),
            jax.ShapeDtypeStruct((share, HD), F32),
            jax.ShapeDtypeStruct((4, HD, 2 * HD), BF),
            jax.ShapeDtypeStruct((HD, 2 * HD), BF),
            jax.ShapeDtypeStruct((HD, 2 * HD), BF),
        ],
        compiler_params=pltpu.CompilerParams(vmem_limit_bytes=SMALL),
        cost_estimate=pl.CostEstimate(flops=900_000_000, bytes_accessed=5_000_000, transcendentals=0),
        name="prep",
    )(
        pos,
        *(
            pltpu.with_memory_space_constraint(array, pltpu.HBM)
            for array in (
                out_weight,
                latent_weight,
                hidden,
                query_weight,
                key_weight,
                query_gain.reshape(1, -1),
                key_gain.reshape(1, -1),
                query_weight,
                key_weight,
            )
        ),
    )


def low_kernel(pos, p0, p1, p2, p3, kv0, kv1, kv2, kv3, w2, hl, out, q_s, part_s):
    z = pos[1]
    for shift, piece in enumerate((p0, p1, p2, p3)):
        q_s[lax.rem(z + 4 - shift, 4)] = piece[:, 0:HD]
    for half in range(2):
        q = q_s[2 * half : 2 * half + 2].reshape(2 * TOK, HD)
        blocks = (kv0, kv1, kv2, kv3)
        scores = [dot_nt(q, kv[:, 0:HD]) * SCALE for kv in blocks]
        top = functools.reduce(jnp.maximum, [jnp.max(s, axis=1, keepdims=True) for s in scores])
        total = jnp.zeros((2 * TOK, 1), F32)
        numerator = jnp.zeros((2 * TOK, HD), F32)
        for s, kv in zip(scores, blocks):
            e = jnp.exp2(s - top)
            total = total + jnp.sum(e, axis=1, keepdims=True)
            numerator = numerator + dot(e.astype(BF), kv[:, HD : 2 * HD])
        attn = (numerator / total).astype(BF)
        part_s[2 * half * TOK : (2 * half + 2) * TOK, :] = dot2(attn, w2[...])
    share = TOK // 8
    rows = pl.ds(pl.multiple_of(z * TOK + pos[3] * share, share), share)
    part_s[rows, :] = part_s[rows, :] + hl[...]
    out[...] = part_s[...].astype(BF)


def low_attention(pos, pieces, kvs, w2, hl):
    args = (*pieces, *kvs, w2, hl)
    return pl.pallas_call(
        low_kernel,
        grid_spec=pltpu.PrefetchScalarGridSpec(
            num_scalar_prefetch=1,
            grid=(1,),
            in_specs=[whole(a.shape) for a in args],
            out_specs=whole((4 * TOK, HD)),
            scratch_shapes=[pltpu.VMEM((4, TOK, HD), BF), pltpu.VMEM((4 * TOK, HD), F32)],
        ),
        out_shape=pltpu.VMEM((4 * TOK, HD), BF),
        compiler_params=pltpu.CompilerParams(vmem_limit_bytes=2 * SMALL),
        name="low",
    )(pos, *args)


CHUNK = 4
BLOCK = 2048
TINY = 2.0**-90


def hi_kernel(
    pos,
    lat0,
    lat1,
    lat2,
    lat3,
    conv_hbm,
    b1,
    second,
    b2,
    gq,
    gk,
    m,
    wv,
    attn_out,
    up_out,
    grid_s,
    lat_s,
    key_s,
    val_s,
    q_s,
    nat_s,
    acc_s,
    bound_s,
    conv,
    conv_sem,
):
    x, z, c, g = pos[0], pos[1], pos[2], pos[3]
    fetch = pltpu.make_async_copy(conv_hbm, conv, conv_sem)
    fetch.start()
    for dx, dc, piece in ((0, 0, lat0), (0, 1, lat1), (1, 0, lat2), (1, 1, lat3)):
        px = lax.bitwise_xor(x, dx)
        pc = lax.bitwise_xor(c, dc)
        for pz in range(4):
            lat_s[px * 8 + pz * 2 + pc] = piece[pz * TOK : (pz + 1) * TOK, :]
    grid_s[...] = jnp.zeros_like(grid_s)
    lat = lat_s[...].reshape(FRAMES * TOK, HD).astype(F32)
    column = lax.rem(lax.broadcasted_iota(jnp.int32, (FRAMES * TOK, HD), 0), W_LO)
    left = jnp.where(column == 0, 0.0, pltpu.roll(lat, 1, 0))
    right = jnp.where(column == W_LO - 1, 0.0, pltpu.roll(lat, FRAMES * TOK - 1, 0))
    for index, shifted in enumerate((left, lat, right)):
        grid_s[index, 1 : FRAMES + 1, 1 : H_LO + 1] = shifted.astype(BF).reshape(FRAMES, H_LO, W_LO, HD)

    val_s[:, HD : 2 * HD] = jnp.ones((KEYS, HD), BF)
    fetch.wait()
    biggest = jnp.zeros((1, 1), F32)
    rows = CHUNK * TOK
    for first in range(0, FRAMES, CHUNK):
        taps = []
        for a in range(3):
            for b in range(3):
                for t in range(3):
                    taps.append(grid_s[t, first + a : first + a + CHUNK, b : b + H_LO].reshape(rows, HD))
        middle = dot(jnp.concatenate(taps, axis=1), conv[...]) + b1[...]
        middle = (middle * (0.5 * jnp.tanh(0.5 * middle) + 0.5)).astype(BF)
        sub = dot(middle, second[...]) + b2[...]
        base = lat_s[first : first + CHUNK].reshape(rows, HD).astype(F32)
        for s in range(4):
            up = (sub[:, s * HD : (s + 1) * HD] + base).astype(BF)
            upf = up.astype(F32)
            square = jnp.sum(dot2(up, gk[...]) * upf, axis=1, keepdims=True)
            inverse = lax.rsqrt(jnp.maximum(square, 0.0) * (1.0 / 4096.0) + 1e-6)
            key = (upf * inverse).astype(BF)
            where = pl.ds(s * FRAMES * TOK + first * TOK, rows)
            val_s[where, 0:HD] = up
            key_s[where, :] = key
            keyf = key.astype(F32)
            length = jnp.sum(keyf * keyf, axis=1, keepdims=True)
            biggest = jnp.maximum(biggest, jnp.max(length, axis=0, keepdims=True))

    frame = x * 8 + z * 2 + c
    own = jnp.concatenate(
        [val_s[pl.ds(pl.multiple_of(s * FRAMES * TOK + frame * TOK, TOK), TOK), 0:HD] for s in range(4)], axis=0
    )
    to = lax.broadcasted_iota(jnp.int32, (4 * TOK, 4 * TOK), 0)
    source = lax.broadcasted_iota(jnp.int32, (4 * TOK, 4 * TOK), 1)
    p, r = (to >> 6) & 1, to & 1
    wanted = (((p << 1) | r) << 7) | ((to >> 7) << 5) | ((to >> 1) & (W_LO - 1))
    natural = dot(jnp.where(source == wanted, 1.0, 0.0).astype(BF), own)
    nat_s[...] = natural
    up_out[...] = nat_s[pl.ds(pl.multiple_of(g * 2 * W_LO, 2 * W_LO), 2 * W_LO), :].astype(BF)
    mine = natural.astype(BF)
    square = jnp.sum(dot2(mine, gq[...]) * natural, axis=1, keepdims=True)
    inverse = lax.rsqrt(jnp.maximum(square, 0.0) * (1.0 / 4096.0) + 1e-6) * SCALE
    for head in range(4):
        q_s[head] = (dot2(mine, m[head]) * inverse).astype(BF)

    for head in range(4):
        qf = q_s[head].astype(F32)
        bound = jnp.sqrt(jnp.sum(qf * qf, axis=1, keepdims=True) * biggest)
        bound_s[head] = jnp.broadcast_to(bound, (4 * TOK, HD))
    acc_s[...] = jnp.zeros_like(acc_s)

    def step(j, carry):
        keys = pl.ds(pl.multiple_of(j * BLOCK, BLOCK), BLOCK)
        for head in range(4):
            scores = dot_nt(q_s[head], key_s[keys, :])
            weights = jnp.exp2(scores - bound_s[head, :, 0:1]).astype(BF)
            acc_s[head] += dot(weights, val_s[keys, :])
        return carry

    lax.fori_loop(0, KEYS // BLOCK, step, 0)

    @pl.when(jnp.logical_not(jnp.min(acc_s[:, :, HD:]) > TINY))
    def _():
        def careful_head(head, carry):
            acc_s[head] = jnp.zeros((4 * TOK, 2 * HD), F32)
            bound_s[head] = jnp.full((4 * TOK, HD), -1e30, F32)

            def careful(j, carry):
                keys = pl.ds(pl.multiple_of(j * 512, 512), 512)
                scores = dot_nt(q_s[head], key_s[keys, :])
                before = bound_s[head, :, 0:1]
                top = jnp.maximum(before, jnp.max(scores, axis=1, keepdims=True))
                weights = jnp.exp2(scores - top).astype(BF)
                acc_s[head] = acc_s[head] * jnp.exp2(before - top) + dot(weights, val_s[keys, :])
                bound_s[head] = jnp.broadcast_to(top, (4 * TOK, HD))
                return carry

            return lax.fori_loop(0, KEYS // 512, careful, carry)

        lax.fori_loop(0, 4, careful_head, 0)

    for head in range(4):
        mixed = (acc_s[head, :, :HD] / acc_s[head, :, HD:]).astype(BF)
        columns = slice(head * HD, (head + 1) * HD)
        attn_out[:, columns] = dot(mixed, wv[:, columns]).astype(BF)


def hi_attention(pos, lats, conv_first, bias_first, conv_second, bias_second, gq, gk, m, value_weight):
    mid = conv_second.shape[0]
    conv = conv_first.reshape(27 * HD, mid)
    args = (*lats, conv, bias_first.reshape(1, -1), conv_second, bias_second.reshape(1, -1), gq, gk, m, value_weight)
    in_specs = [whole(a.shape) for a in args]
    in_specs[-1] = pl.BlockSpec((HD, 4 * HD), lambda i, pos: (0, pos[3]))
    in_specs[len(lats)] = pl.BlockSpec(memory_space=pltpu.HBM)
    return pl.pallas_call(
        hi_kernel,
        grid_spec=pltpu.PrefetchScalarGridSpec(
            num_scalar_prefetch=1,
            grid=(1,),
            in_specs=in_specs,
            out_specs=[whole((4 * TOK, 4 * HD)), whole((2 * W_LO, HD))],
            scratch_shapes=[
                pltpu.VMEM((3, FRAMES + 2, H_LO + 2, W_LO, HD), BF),
                pltpu.VMEM((FRAMES, TOK, HD), BF),
                pltpu.VMEM((KEYS, HD), BF),
                pltpu.VMEM((KEYS, 2 * HD), BF),
                pltpu.VMEM((4, 4 * TOK, HD), BF),
                pltpu.VMEM((4 * TOK, HD), F32),
                pltpu.VMEM((4, 4 * TOK, 2 * HD), F32),
                pltpu.VMEM((4, 4 * TOK, HD), F32),
                pltpu.VMEM(conv.shape, BF),
                pltpu.SemaphoreType.DMA,
            ],
        ),
        out_shape=[
            jax.ShapeDtypeStruct((4 * TOK, 4 * HD), BF),
            jax.ShapeDtypeStruct((2 * W_LO, HD), BF),
        ],
        compiler_params=pltpu.CompilerParams(vmem_limit_bytes=LARGE),
        name="hi",
    )(pos, *args)


def z_shift(step):
    return [(i, (i & 9) | ((((i >> 1) + step) & 3) << 1)) for i in range(16)]


def trade(value, partner):
    pairs = []
    for seq in range(16):
        for head in range(8):
            x, y, z, core = (seq >> 3) * 2 + (head & 1), head >> 1, (seq >> 1) & 3, seq & 1
            x, y, z, core = partner(x, y, z, core)
            other = ((x >> 1) * 8 + z * 2 + core) * 8 + y * 2 + (x & 1)
            pairs.append((seq * 8 + head, other))
    return lax.ppermute(value, ("seq", "head"), pairs)


def to_core(x, y, z, core):
    return x, y, z, core ^ 1


def to_x_far(x, y, z, core):
    return x ^ 2, y, z, core


def to_x_near(x, y, z, core):
    return x ^ 3, y, z, core


HOPS = (("x", 1), ("y", 1), ("y", 3), ("z", 1), ("z", 3))


def sum_step(step):
    def partner(x, y, z, core):
        axis, bit = HOPS[(step + core) % 5]
        if axis == "x":
            return x ^ bit, y, z, core
        if axis == "y":
            return x, y ^ bit, z, core
        return x, y, z ^ bit, core

    return partner


def local(
    hidden_low,
    query_low,
    key_low,
    value_low,
    out_weight,
    latent_weight,
    conv_first,
    bias_first,
    conv_second,
    bias_second,
    query_weight,
    key_weight,
    value_weight,
    query_gain,
    key_gain,
):
    seq, head = lax.axis_index("seq"), lax.axis_index("head")
    pos = jnp.stack([seq // 8, (seq // 2) % 4, seq % 2, head]).astype(jnp.int32)
    pieces = pack(pos, query_low, key_low, value_low)
    pieces = [pieces[0]] + [
        lax.ppermute(pieces[step], "seq", z_shift(step)) for step in (1, 2, 3)
    ]
    w2, hl, m, gq, gk = prep(
        pos, out_weight, latent_weight, hidden_low, query_weight, key_weight, query_gain, key_gain
    )
    kv = jnp.concatenate([piece[:, HD:] for piece in pieces], axis=0)
    kv_x = trade(kv, to_x_far)
    kv_c = trade(kv, to_core)
    kv_x, w2, hl, m, gq, gk = lax.optimization_barrier((kv_x, w2, hl, m, gq, gk))
    kv_xc = trade(kv_x, to_core)
    latent = low_attention(pos, pieces, (kv, kv_c, kv_x, kv_xc), w2, hl)
    for step in range(5):
        latent = (latent.astype(F32) + trade(latent, sum_step(step)).astype(F32)).astype(BF)
    lat_x = trade(latent, to_x_near)
    lat_c = trade(latent, to_core)
    lat_xc = trade(lat_x, to_core)
    attn, up = hi_attention(
        pos,
        (latent, lat_c, lat_x, lat_xc),
        conv_first,
        bias_first,
        conv_second,
        bias_second,
        gq,
        gk,
        m,
        value_weight,
    )
    return attn, up


def solution(mesh):
    placed = (
        P("seq", None),
        P("seq", "head"),
        P("seq", "head"),
        P("seq", "head"),
        P("head", None),
    ) + (P(),) * 10
    return jax.shard_map(
        local,
        mesh=mesh,
        in_specs=placed,
        out_specs=(P("seq", "head"), P(("seq", "head"), None)),
        check_vma=False,
    )
```

```python
import functools
import math

import jax
import jax.numpy as jnp
from jax import lax
from jax.experimental import pallas as pl
from jax.experimental.pallas import tpu as pltpu
from jax.sharding import PartitionSpec as P

HD = 128
H_LO = 4
W_LO = 32
FRAMES = 16
TOK = H_LO * W_LO
KEYS = 4 * FRAMES * TOK
LOG2E = 1.4426950408889634
SCALE = LOG2E / math.sqrt(HD)
BF = jnp.bfloat16
F32 = jnp.float32
SMALL, LARGE = 16 * 2**20, 46 * 2**20
NT = (((1,), (1,)), ((), ()))


def dot(a, b):
    return jnp.dot(a, b, preferred_element_type=F32)


def dot_nt(a, b):
    return lax.dot_general(a, b, NT, preferred_element_type=F32)


def split2(x):
    high = x.astype(BF)
    low = (x - high.astype(F32)).astype(BF)
    return jnp.concatenate([high, low], axis=1)


def dot2(a, b2):
    both = dot(a, b2)
    half = both.shape[1] // 2
    return both[:, :half] + both[:, half:]


def whole(shape):
    return pl.BlockSpec(shape, lambda *_: (0,) * len(shape))


def pack_kernel(q_ref, k_ref, v_ref, *outs):
    z = (lax.axis_index("seq") >> 1) & 3
    for shift, out in enumerate(outs):
        head = (z + shift) & 3
        columns = pl.ds(pl.multiple_of(head * HD, HD), HD)
        out[:, 0:HD] = q_ref[:, columns]
        out[:, HD : 2 * HD] = k_ref[:, columns]
        out[:, 2 * HD : 3 * HD] = v_ref[:, columns]


def pack(q, k, v):
    return pl.pallas_call(
        pack_kernel,
        out_shape=[pltpu.VMEM((TOK, 3 * HD), BF)] * 4,
        compiler_params=pltpu.CompilerParams(vmem_limit_bytes=SMALL),
        name="pack",
    )(*(pltpu.with_memory_space_constraint(array, pltpu.HBM) for array in (q, k, v)))


def prep_kernel(pos, ow, lw, hid, wqh, wkh, gq, gk, wq, wk, w2_out, hl_out, m_out, gq_out, gk_out):
    del pos
    w2_out[...] = split2(dot(ow[...], lw[...]))
    hl_out[...] = dot(hid[...], lw[...])
    gain = gq[...] * gk[...]
    for head in range(4):
        cols = slice(head * HD, (head + 1) * HD)
        left = split2(wqh[:, cols].astype(F32) * gain[:, cols])
        right = wkh[:, cols]
        m_out[head] = split2(dot_nt(left[:, :HD], right) + dot_nt(left[:, HD:], right))
    gq_out[...] = split2(dot_nt(wq[...], wq[...]))
    gk_out[...] = split2(dot_nt(wk[...], wk[...]))


def prep(pos, out_weight, latent_weight, hidden, query_weight, key_weight, query_gain, key_gain):
    width = hidden.shape[1]
    share = TOK // 8
    group = 4 * HD
    return pl.pallas_call(
        prep_kernel,
        grid_spec=pltpu.PrefetchScalarGridSpec(
            num_scalar_prefetch=1,
            grid=(1,),
            in_specs=[
                pl.BlockSpec((HD, width), lambda i, pos: (pos[1], 0)),
                whole(latent_weight.shape),
                pl.BlockSpec((share, width), lambda i, pos: (pos[3], 0)),
                pl.BlockSpec((HD, group), lambda i, pos: (0, pos[3])),
                pl.BlockSpec((HD, group), lambda i, pos: (0, pos[3])),
                pl.BlockSpec((1, group), lambda i, pos: (0, pos[3])),
                pl.BlockSpec((1, group), lambda i, pos: (0, pos[3])),
                whole(query_weight.shape),
                whole(key_weight.shape),
            ],
            out_specs=[
                whole((HD, 2 * HD)),
                whole((share, HD)),
                whole((4, HD, 2 * HD)),
                whole((HD, 2 * HD)),
                whole((HD, 2 * HD)),
            ],
        ),
        out_shape=[
            jax.ShapeDtypeStruct((HD, 2 * HD), BF),
            jax.ShapeDtypeStruct((share, HD), F32),
            jax.ShapeDtypeStruct((4, HD, 2 * HD), BF),
            jax.ShapeDtypeStruct((HD, 2 * HD), BF),
            jax.ShapeDtypeStruct((HD, 2 * HD), BF),
        ],
        compiler_params=pltpu.CompilerParams(vmem_limit_bytes=SMALL),
        cost_estimate=pl.CostEstimate(flops=900_000_000, bytes_accessed=5_000_000, transcendentals=0),
        name="prep",
    )(
        pos,
        *(
            pltpu.with_memory_space_constraint(array, pltpu.HBM)
            for array in (
                out_weight,
                latent_weight,
                hidden,
                query_weight,
                key_weight,
                query_gain.reshape(1, -1),
                key_gain.reshape(1, -1),
                query_weight,
                key_weight,
            )
        ),
    )


def low_kernel(pos, p0, p1, p2, p3, kv0, kv1, kv2, kv3, w2, hl, out, q_s, part_s):
    z = pos[1]
    for shift, piece in enumerate((p0, p1, p2, p3)):
        q_s[lax.rem(z + 4 - shift, 4)] = piece[:, 0:HD]
    for half in range(2):
        q = q_s[2 * half : 2 * half + 2].reshape(2 * TOK, HD)
        blocks = (kv0, kv1, kv2, kv3)
        scores = [dot_nt(q, kv[:, 0:HD]) * SCALE for kv in blocks]
        top = functools.reduce(jnp.maximum, [jnp.max(s, axis=1, keepdims=True) for s in scores])
        total = jnp.zeros((2 * TOK, 1), F32)
        numerator = jnp.zeros((2 * TOK, HD), F32)
        for s, kv in zip(scores, blocks):
            e = jnp.exp2(s - top)
            total = total + jnp.sum(e, axis=1, keepdims=True)
            numerator = numerator + dot(e.astype(BF), kv[:, HD : 2 * HD])
        attn = (numerator / total).astype(BF)
        part_s[2 * half * TOK : (2 * half + 2) * TOK, :] = dot2(attn, w2[...])
    share = TOK // 8
    rows = pl.ds(pl.multiple_of(z * TOK + pos[3] * share, share), share)
    part_s[rows, :] = part_s[rows, :] + hl[...]
    out[...] = part_s[...].astype(BF)


def low_attention(pos, pieces, kvs, w2, hl):
    args = (*pieces, *kvs, w2, hl)
    return pl.pallas_call(
        low_kernel,
        grid_spec=pltpu.PrefetchScalarGridSpec(
            num_scalar_prefetch=1,
            grid=(1,),
            in_specs=[whole(a.shape) for a in args],
            out_specs=whole((4 * TOK, HD)),
            scratch_shapes=[pltpu.VMEM((4, TOK, HD), BF), pltpu.VMEM((4 * TOK, HD), F32)],
        ),
        out_shape=pltpu.VMEM((4 * TOK, HD), BF),
        compiler_params=pltpu.CompilerParams(vmem_limit_bytes=2 * SMALL),
        name="low",
    )(pos, *args)


CHUNK = 4
BLOCK = 2048
TINY = 2.0**-90


def hi_kernel(
    pos,
    lat0,
    lat1,
    lat2,
    lat3,
    conv,
    b1,
    second,
    b2,
    gq,
    gk,
    m,
    wv,
    attn_out,
    up_out,
    grid_s,
    lat_s,
    key_s,
    val_s,
    q_s,
    nat_s,
    acc_s,
    bound_s,
):
    x, z, c, g = pos[0], pos[1], pos[2], pos[3]
    for dx, dc, piece in ((0, 0, lat0), (0, 1, lat1), (1, 0, lat2), (1, 1, lat3)):
        px = lax.bitwise_xor(x, dx)
        pc = lax.bitwise_xor(c, dc)
        for pz in range(4):
            lat_s[px * 8 + pz * 2 + pc] = piece[pz * TOK : (pz + 1) * TOK, :]
    edge = jnp.zeros((3, 1, H_LO + 2, W_LO, HD), BF)
    grid_s[:, 0:1] = edge
    grid_s[:, FRAMES + 1 : FRAMES + 2] = edge
    edge = jnp.zeros((3, FRAMES + 2, 1, W_LO, HD), BF)
    grid_s[:, :, 0:1] = edge
    grid_s[:, :, H_LO + 1 : H_LO + 2] = edge
    lat = lat_s[...].reshape(FRAMES * TOK, HD).astype(F32)
    column = lax.rem(lax.broadcasted_iota(jnp.int32, (FRAMES * TOK, HD), 0), W_LO)
    left = jnp.where(column == 0, 0.0, pltpu.roll(lat, 1, 0))
    right = jnp.where(column == W_LO - 1, 0.0, pltpu.roll(lat, FRAMES * TOK - 1, 0))
    for index, shifted in enumerate((left, lat, right)):
        grid_s[index, 1 : FRAMES + 1, 1 : H_LO + 1] = shifted.astype(BF).reshape(FRAMES, H_LO, W_LO, HD)

    val_s[:, HD : 2 * HD] = jnp.ones((KEYS, HD), BF)
    biggest = jnp.zeros((1, 1), F32)
    rows = CHUNK * TOK
    for first in range(0, FRAMES, CHUNK):
        taps = []
        for a in range(3):
            for b in range(3):
                for t in range(3):
                    taps.append(grid_s[t, first + a : first + a + CHUNK, b : b + H_LO].reshape(rows, HD))
        middle = dot(jnp.concatenate(taps, axis=1), conv[...]) + b1[...]
        middle = (middle * (0.5 * jnp.tanh(0.5 * middle) + 0.5)).astype(BF)
        sub = dot(middle, second[...]) + b2[...]
        base = lat_s[first : first + CHUNK].reshape(rows, HD).astype(F32)
        for s in range(4):
            up = (sub[:, s * HD : (s + 1) * HD] + base).astype(BF)
            upf = up.astype(F32)
            square = jnp.sum(dot2(up, gk[...]) * upf, axis=1, keepdims=True)
            inverse = lax.rsqrt(jnp.maximum(square, 0.0) * (1.0 / 4096.0) + 1e-6)
            key = (upf * inverse).astype(BF)
            where = pl.ds(s * FRAMES * TOK + first * TOK, rows)
            val_s[where, 0:HD] = up
            key_s[where, :] = key
            keyf = key.astype(F32)
            length = jnp.sum(keyf * keyf, axis=1, keepdims=True)
            biggest = jnp.maximum(biggest, jnp.max(length, axis=0, keepdims=True))

    frame = x * 8 + z * 2 + c
    own = jnp.concatenate(
        [val_s[pl.ds(pl.multiple_of(s * FRAMES * TOK + frame * TOK, TOK), TOK), 0:HD] for s in range(4)], axis=0
    )
    to = lax.broadcasted_iota(jnp.int32, (4 * TOK, 4 * TOK), 0)
    source = lax.broadcasted_iota(jnp.int32, (4 * TOK, 4 * TOK), 1)
    p, r = (to >> 6) & 1, to & 1
    wanted = (((p << 1) | r) << 7) | ((to >> 7) << 5) | ((to >> 1) & (W_LO - 1))
    natural = dot(jnp.where(source == wanted, 1.0, 0.0).astype(BF), own)
    nat_s[...] = natural
    up_out[...] = nat_s[pl.ds(pl.multiple_of(g * 2 * W_LO, 2 * W_LO), 2 * W_LO), :].astype(BF)
    mine = natural.astype(BF)
    square = jnp.sum(dot2(mine, gq[...]) * natural, axis=1, keepdims=True)
    inverse = lax.rsqrt(jnp.maximum(square, 0.0) * (1.0 / 4096.0) + 1e-6) * SCALE
    for head in range(4):
        q_s[head] = (dot2(mine, m[head]) * inverse).astype(BF)

    for head in range(4):
        qf = q_s[head].astype(F32)
        bound = jnp.sqrt(jnp.sum(qf * qf, axis=1, keepdims=True) * biggest)
        bound_s[head] = jnp.broadcast_to(bound, (4 * TOK, HD))
    acc_s[...] = jnp.zeros_like(acc_s)

    def step(j, carry):
        keys = pl.ds(pl.multiple_of(j * BLOCK, BLOCK), BLOCK)
        for head in range(4):
            scores = dot_nt(q_s[head], key_s[keys, :])
            weights = jnp.exp2(scores - bound_s[head, :, 0:1]).astype(BF)
            acc_s[head] += dot(weights, val_s[keys, :])
        return carry

    lax.fori_loop(0, KEYS // BLOCK, step, 0, unroll=2)

    @pl.when(jnp.logical_not(jnp.min(acc_s[:, :, HD:]) > TINY))
    def _():
        def careful_head(head, carry):
            acc_s[head] = jnp.zeros((4 * TOK, 2 * HD), F32)
            bound_s[head] = jnp.full((4 * TOK, HD), -1e30, F32)

            def careful(j, carry):
                keys = pl.ds(pl.multiple_of(j * 512, 512), 512)
                scores = dot_nt(q_s[head], key_s[keys, :])
                before = bound_s[head, :, 0:1]
                top = jnp.maximum(before, jnp.max(scores, axis=1, keepdims=True))
                weights = jnp.exp2(scores - top).astype(BF)
                acc_s[head] = acc_s[head] * jnp.exp2(before - top) + dot(weights, val_s[keys, :])
                bound_s[head] = jnp.broadcast_to(top, (4 * TOK, HD))
                return carry

            return lax.fori_loop(0, KEYS // 512, careful, carry)

        lax.fori_loop(0, 4, careful_head, 0)

    for head in range(4):
        mixed = (acc_s[head, :, :HD] / acc_s[head, :, HD:]).astype(BF)
        columns = slice(head * HD, (head + 1) * HD)
        attn_out[:, columns] = dot(mixed, wv[:, columns]).astype(BF)


def hi_attention(pos, lats, conv_first, bias_first, conv_second, bias_second, gq, gk, m, value_weight):
    mid = conv_second.shape[0]
    conv = conv_first.reshape(27 * HD, mid)
    args = (*lats, conv, bias_first.reshape(1, -1), conv_second, bias_second.reshape(1, -1), gq, gk, m, value_weight)
    in_specs = [whole(a.shape) for a in args]
    in_specs[-1] = pl.BlockSpec((HD, 4 * HD), lambda i, pos: (0, pos[3]))
    return pl.pallas_call(
        hi_kernel,
        grid_spec=pltpu.PrefetchScalarGridSpec(
            num_scalar_prefetch=1,
            grid=(1,),
            in_specs=in_specs,
            out_specs=[whole((4 * TOK, 4 * HD)), whole((2 * W_LO, HD))],
            scratch_shapes=[
                pltpu.VMEM((3, FRAMES + 2, H_LO + 2, W_LO, HD), BF),
                pltpu.VMEM((FRAMES, TOK, HD), BF),
                pltpu.VMEM((KEYS, HD), BF),
                pltpu.VMEM((KEYS, 2 * HD), BF),
                pltpu.VMEM((4, 4 * TOK, HD), BF),
                pltpu.VMEM((4 * TOK, HD), F32),
                pltpu.VMEM((4, 4 * TOK, 2 * HD), F32),
                pltpu.VMEM((4, 4 * TOK, HD), F32),
            ],
        ),
        out_shape=[
            jax.ShapeDtypeStruct((4 * TOK, 4 * HD), BF),
            jax.ShapeDtypeStruct((2 * W_LO, HD), BF),
        ],
        compiler_params=pltpu.CompilerParams(vmem_limit_bytes=LARGE),
        name="hi",
    )(pos, *args)


def z_shift(step):
    return [(i, (i & 9) | ((((i >> 1) + step) & 3) << 1)) for i in range(16)]


def trade(value, partner):
    pairs = []
    for seq in range(16):
        for head in range(8):
            x, y, z, core = (seq >> 3) * 2 + (head & 1), head >> 1, (seq >> 1) & 3, seq & 1
            x, y, z, core = partner(x, y, z, core)
            other = ((x >> 1) * 8 + z * 2 + core) * 8 + y * 2 + (x & 1)
            pairs.append((seq * 8 + head, other))
    return lax.ppermute(value, ("seq", "head"), pairs)


def to_core(x, y, z, core):
    return x, y, z, core ^ 1


def to_x_far(x, y, z, core):
    return x ^ 2, y, z, core


def to_x_near(x, y, z, core):
    return x ^ 3, y, z, core


ROUNDS = ((("x", "x"), (1,)), (("y", "z"), (1, 3, 2)), (("z", "y"), (1, 3, 2)))


def along(axes, bit):
    def partner(x, y, z, core):
        flip = {"x": 0, "y": 0, "z": 0, axes[core]: bit}
        return x ^ flip["x"], y ^ flip["y"], z ^ flip["z"], core

    return partner


def sum_round(value, axes, bits):
    arrived = [trade(value, along(axes, bit)).astype(F32) for bit in bits]
    return sum(arrived, value.astype(F32)).astype(BF)


def local(
    hidden_low,
    query_low,
    key_low,
    value_low,
    out_weight,
    latent_weight,
    conv_first,
    bias_first,
    conv_second,
    bias_second,
    query_weight,
    key_weight,
    value_weight,
    query_gain,
    key_gain,
):
    seq, head = lax.axis_index("seq"), lax.axis_index("head")
    pos = jnp.stack([seq // 8, (seq // 2) % 4, seq % 2, head]).astype(jnp.int32)
    pieces = pack(query_low, key_low, value_low)
    pieces = [pieces[0]] + [
        lax.ppermute(pieces[step], "seq", z_shift(step)) for step in (1, 2, 3)
    ]
    w2, hl, m, gq, gk = prep(
        pos, out_weight, latent_weight, hidden_low, query_weight, key_weight, query_gain, key_gain
    )
    kv = jnp.concatenate([piece[:, HD:] for piece in pieces], axis=0)
    kv_x = trade(kv, to_x_far)
    kv_c = trade(kv, to_core)
    kv_x, w2, hl, m, gq, gk = lax.optimization_barrier((kv_x, w2, hl, m, gq, gk))
    kv_xc = trade(kv_x, to_core)
    latent = low_attention(pos, pieces, (kv, kv_c, kv_x, kv_xc), w2, hl)
    for axes, bits in ROUNDS:
        latent = sum_round(latent, axes, bits)
    lat_x = trade(latent, to_x_near)
    lat_c = trade(latent, to_core)
    lat_xc = trade(lat_x, to_core)
    attn, up = hi_attention(
        pos,
        (latent, lat_c, lat_x, lat_xc),
        conv_first,
        bias_first,
        conv_second,
        bias_second,
        gq,
        gk,
        m,
        value_weight,
    )
    return attn, up


def solution(mesh):
    placed = (
        P("seq", None),
        P("seq", "head"),
        P("seq", "head"),
        P("seq", "head"),
        P("head", None),
    ) + (P(),) * 10
    return jax.shard_map(
        local,
        mesh=mesh,
        in_specs=placed,
        out_specs=(P("seq", "head"), P(("seq", "head"), None)),
        check_vma=False,
    )
```

```python
import functools
import math

import jax
import jax.numpy as jnp
from jax import lax
from jax.experimental import pallas as pl
from jax.experimental.pallas import tpu as pltpu
from jax.sharding import PartitionSpec as P

HD = 128
H_LO = 4
W_LO = 32
FRAMES = 16
TOK = H_LO * W_LO
KEYS = 4 * FRAMES * TOK
LOG2E = 1.4426950408889634
SCALE = LOG2E / math.sqrt(HD)
BF = jnp.bfloat16
F32 = jnp.float32
SMALL, LARGE = 16 * 2**20, 46 * 2**20
NT = (((1,), (1,)), ((), ()))


def dot(a, b):
    return jnp.dot(a, b, preferred_element_type=F32)


def dot_nt(a, b):
    return lax.dot_general(a, b, NT, preferred_element_type=F32)


def split2(x):
    high = x.astype(BF)
    low = (x - high.astype(F32)).astype(BF)
    return jnp.concatenate([high, low], axis=1)


def dot2(a, b2):
    both = dot(a, b2)
    half = both.shape[1] // 2
    return both[:, :half] + both[:, half:]


def whole(shape):
    return pl.BlockSpec(shape, lambda *_: (0,) * len(shape))


def pack_kernel(q_ref, k_ref, v_ref, *outs):
    z = (lax.axis_index("seq") >> 1) & 3
    for shift, out in enumerate(outs):
        head = (z + shift) & 3
        columns = pl.ds(pl.multiple_of(head * HD, HD), HD)
        out[:, 0:HD] = q_ref[:, columns]
        out[:, HD : 2 * HD] = k_ref[:, columns]
        out[:, 2 * HD : 3 * HD] = v_ref[:, columns]


def pack(q, k, v):
    return pl.pallas_call(
        pack_kernel,
        out_shape=[pltpu.VMEM((TOK, 3 * HD), BF)] * 4,
        compiler_params=pltpu.CompilerParams(vmem_limit_bytes=SMALL),
        name="pack",
    )(*(pltpu.with_memory_space_constraint(array, pltpu.HBM) for array in (q, k, v)))


def prep_kernel(pos, ow, lw, hid, wqh, wkh, gq, gk, wq, wk, w2_out, hl_out, m_out, gq_out, gk_out):
    del pos
    w2_out[...] = split2(dot(ow[...], lw[...]))
    hl_out[...] = dot(hid[...], lw[...])
    gain = gq[...] * gk[...]
    for head in range(4):
        cols = slice(head * HD, (head + 1) * HD)
        left = split2(wqh[:, cols].astype(F32) * gain[:, cols])
        right = wkh[:, cols]
        m_out[head] = split2(dot_nt(left[:, :HD], right) + dot_nt(left[:, HD:], right))
    gq_out[...] = split2(dot_nt(wq[...], wq[...]))
    gk_out[...] = split2(dot_nt(wk[...], wk[...]))


def prep(pos, out_weight, latent_weight, hidden, query_weight, key_weight, query_gain, key_gain):
    width = hidden.shape[1]
    share = TOK // 8
    group = 4 * HD
    return pl.pallas_call(
        prep_kernel,
        grid_spec=pltpu.PrefetchScalarGridSpec(
            num_scalar_prefetch=1,
            grid=(1,),
            in_specs=[
                pl.BlockSpec((HD, width), lambda i, pos: (pos[1], 0)),
                whole(latent_weight.shape),
                pl.BlockSpec((share, width), lambda i, pos: (pos[3], 0)),
                pl.BlockSpec((HD, group), lambda i, pos: (0, pos[3])),
                pl.BlockSpec((HD, group), lambda i, pos: (0, pos[3])),
                pl.BlockSpec((1, group), lambda i, pos: (0, pos[3])),
                pl.BlockSpec((1, group), lambda i, pos: (0, pos[3])),
                whole(query_weight.shape),
                whole(key_weight.shape),
            ],
            out_specs=[
                whole((HD, 2 * HD)),
                whole((share, HD)),
                whole((4, HD, 2 * HD)),
                whole((HD, 2 * HD)),
                whole((HD, 2 * HD)),
            ],
        ),
        out_shape=[
            jax.ShapeDtypeStruct((HD, 2 * HD), BF),
            jax.ShapeDtypeStruct((share, HD), F32),
            jax.ShapeDtypeStruct((4, HD, 2 * HD), BF),
            jax.ShapeDtypeStruct((HD, 2 * HD), BF),
            jax.ShapeDtypeStruct((HD, 2 * HD), BF),
        ],
        compiler_params=pltpu.CompilerParams(vmem_limit_bytes=SMALL),
        cost_estimate=pl.CostEstimate(flops=900_000_000, bytes_accessed=5_000_000, transcendentals=0),
        name="prep",
    )(
        pos,
        *(
            pltpu.with_memory_space_constraint(array, pltpu.HBM)
            for array in (
                out_weight,
                latent_weight,
                hidden,
                query_weight,
                key_weight,
                query_gain.reshape(1, -1),
                key_gain.reshape(1, -1),
                query_weight,
                key_weight,
            )
        ),
    )


def low_kernel(pos, p0, p1, p2, p3, kv0, kv1, kv2, kv3, w2, hl, out, q_s, part_s):
    z = pos[1]
    for shift, piece in enumerate((p0, p1, p2, p3)):
        q_s[lax.rem(z + 4 - shift, 4)] = piece[:, 0:HD]
    for half in range(2):
        q = q_s[2 * half : 2 * half + 2].reshape(2 * TOK, HD)
        blocks = (kv0, kv1, kv2, kv3)
        scores = [dot_nt(q, kv[:, 0:HD]) * SCALE for kv in blocks]
        top = functools.reduce(jnp.maximum, [jnp.max(s, axis=1, keepdims=True) for s in scores])
        total = jnp.zeros((2 * TOK, 1), F32)
        numerator = jnp.zeros((2 * TOK, HD), F32)
        for s, kv in zip(scores, blocks):
            e = jnp.exp2(s - top)
            total = total + jnp.sum(e, axis=1, keepdims=True)
            numerator = numerator + dot(e.astype(BF), kv[:, HD : 2 * HD])
        attn = (numerator / total).astype(BF)
        part_s[2 * half * TOK : (2 * half + 2) * TOK, :] = dot2(attn, w2[...])
    share = TOK // 8
    rows = pl.ds(pl.multiple_of(z * TOK + pos[3] * share, share), share)
    part_s[rows, :] = part_s[rows, :] + hl[...]
    out[...] = part_s[...].astype(BF)


def low_attention(pos, pieces, kvs, w2, hl):
    args = (*pieces, *kvs, w2, hl)
    return pl.pallas_call(
        low_kernel,
        grid_spec=pltpu.PrefetchScalarGridSpec(
            num_scalar_prefetch=1,
            grid=(1,),
            in_specs=[whole(a.shape) for a in args],
            out_specs=whole((4 * TOK, HD)),
            scratch_shapes=[pltpu.VMEM((4, TOK, HD), BF), pltpu.VMEM((4 * TOK, HD), F32)],
        ),
        out_shape=pltpu.VMEM((4 * TOK, HD), BF),
        compiler_params=pltpu.CompilerParams(vmem_limit_bytes=2 * SMALL),
        name="low",
    )(pos, *args)


CHUNK = 4
ROWS = CHUNK * TOK
HALF = FRAMES // 2
BLOCK = 2048
TINY = 2.0**-90


def fill_grid(grid_s, lat_s):
    frames = lat_s.shape[0]
    edge = jnp.zeros((3, 1, H_LO + 2, W_LO, HD), BF)
    grid_s[:, 0:1] = edge
    grid_s[:, frames + 1 : frames + 2] = edge
    edge = jnp.zeros((3, frames + 2, 1, W_LO, HD), BF)
    grid_s[:, :, 0:1] = edge
    grid_s[:, :, H_LO + 1 : H_LO + 2] = edge
    lat = lat_s[...].reshape(frames * TOK, HD).astype(F32)
    column = lax.broadcasted_iota(jnp.int32, (frames * TOK, HD), 0) & (W_LO - 1)
    left = jnp.where(column == 0, 0.0, pltpu.roll(lat, 1, 0))
    right = jnp.where(column == W_LO - 1, 0.0, pltpu.roll(lat, frames * TOK - 1, 0))
    for index, shifted in enumerate((left, lat, right)):
        grid_s[index, 1 : frames + 1, 1 : H_LO + 1] = shifted.astype(BF).reshape(frames, H_LO, W_LO, HD)


def upsample_chunk(first, grid_s, lat_s, conv, b1, second, b2, gk):
    taps = []
    for a in range(3):
        for b in range(3):
            for t in range(3):
                taps.append(grid_s[t, pl.ds(first + a, CHUNK), b : b + H_LO].reshape(ROWS, HD))
    middle = dot(jnp.concatenate(taps, axis=1), conv[...]) + b1[...]
    middle = (middle * (0.5 * jnp.tanh(0.5 * middle) + 0.5)).astype(BF)
    sub = dot(middle, second[...]) + b2[...]
    base = lat_s[pl.ds(first, CHUNK)].reshape(ROWS, HD).astype(F32)
    pairs = []
    longest = jnp.zeros((1, 1), F32)
    for s in range(4):
        up = (sub[:, s * HD : (s + 1) * HD] + base).astype(BF)
        upf = up.astype(F32)
        square = jnp.sum(dot2(up, gk[...]) * upf, axis=1, keepdims=True)
        key = (upf * lax.rsqrt(jnp.maximum(square, 0.0) * (1.0 / 4096.0) + 1e-6)).astype(BF)
        keyf = key.astype(F32)
        length = jnp.sum(keyf * keyf, axis=1, keepdims=True)
        longest = jnp.maximum(longest, jnp.max(length, axis=0, keepdims=True))
        pairs.append((up, key))
    return pairs, longest


def early_kernel(pos, lat0, lat1, conv, b1, second, b2, gk, up_out, key_out, long_out, grid_s, lat_s):
    x, c = pos[0], pos[2]
    for dc, piece in ((0, lat0), (1, lat1)):
        pc = lax.bitwise_xor(c, dc)
        for pz in range(4):
            lat_s[pz * 2 + pc] = piece[pz * TOK : (pz + 1) * TOK, :]
    fill_grid(grid_s, lat_s)
    pairs, longest = upsample_chunk(x * (HALF - CHUNK), grid_s, lat_s, conv, b1, second, b2, gk)
    for s, (up, key) in enumerate(pairs):
        up_out[s] = up
        key_out[s] = key
    long_out[...] = jnp.broadcast_to(longest, long_out.shape)


def early_frames(pos, lats, conv, b1, second, b2, gk):
    args = (*lats, conv, b1, second, b2, gk)
    piece = jax.ShapeDtypeStruct((4, ROWS, HD), BF)
    return pl.pallas_call(
        early_kernel,
        grid_spec=pltpu.PrefetchScalarGridSpec(
            num_scalar_prefetch=1,
            grid=(1,),
            in_specs=[whole(a.shape) for a in args],
            out_specs=[whole(piece.shape), whole(piece.shape), whole((8, HD))],
            scratch_shapes=[
                pltpu.VMEM((3, HALF + 2, H_LO + 2, W_LO, HD), BF),
                pltpu.VMEM((HALF, TOK, HD), BF),
            ],
        ),
        out_shape=[piece, piece, jax.ShapeDtypeStruct((8, HD), F32)],
        compiler_params=pltpu.CompilerParams(vmem_limit_bytes=2 * SMALL),
        cost_estimate=pl.CostEstimate(flops=2_400_000_000, bytes_accessed=6_000_000, transcendentals=300_000),
        name="early",
    )(pos, *args)


def hi_kernel(
    pos,
    lat0,
    lat1,
    lat2,
    lat3,
    up_in,
    key_in,
    long_in,
    conv,
    b1,
    second,
    b2,
    gq,
    gk,
    m,
    wv,
    attn_out,
    up_out,
    grid_s,
    lat_s,
    key_s,
    val_s,
    q_s,
    nat_s,
    acc_s,
    bound_s,
):
    x, z, c, g = pos[0], pos[1], pos[2], pos[3]
    for dx, dc, piece in ((0, 0, lat0), (0, 1, lat1), (1, 0, lat2), (1, 1, lat3)):
        px = lax.bitwise_xor(x, dx)
        pc = lax.bitwise_xor(c, dc)
        for pz in range(4):
            lat_s[px * 8 + pz * 2 + pc] = piece[pz * TOK : (pz + 1) * TOK, :]
    fill_grid(grid_s, lat_s)
    val_s[:, HD : 2 * HD] = jnp.ones((KEYS, HD), BF)

    def keep(first, s, up, key):
        rows = pl.ds(pl.multiple_of(s * FRAMES * TOK + first * TOK, ROWS), ROWS)
        val_s[rows, 0:HD] = up
        key_s[rows, :] = key

    ends = FRAMES - CHUNK
    for s in range(4):
        keep(x * ends, s, up_in[s], key_in[s])
    biggest = long_in[0:1, 0:1]
    for first in (CHUNK, 2 * CHUNK, (1 - x) * ends):
        pairs, longest = upsample_chunk(first, grid_s, lat_s, conv, b1, second, b2, gk)
        biggest = jnp.maximum(biggest, longest)
        for s, (up, key) in enumerate(pairs):
            keep(first, s, up, key)

    frame = x * 8 + z * 2 + c
    own = jnp.concatenate(
        [val_s[pl.ds(pl.multiple_of(s * FRAMES * TOK + frame * TOK, TOK), TOK), 0:HD] for s in range(4)], axis=0
    )
    to = lax.broadcasted_iota(jnp.int32, (4 * TOK, 4 * TOK), 0)
    source = lax.broadcasted_iota(jnp.int32, (4 * TOK, 4 * TOK), 1)
    p, r = (to >> 6) & 1, to & 1
    wanted = (((p << 1) | r) << 7) | ((to >> 7) << 5) | ((to >> 1) & (W_LO - 1))
    natural = dot(jnp.where(source == wanted, 1.0, 0.0).astype(BF), own)
    nat_s[...] = natural
    up_out[...] = nat_s[pl.ds(pl.multiple_of(g * 2 * W_LO, 2 * W_LO), 2 * W_LO), :].astype(BF)
    mine = natural.astype(BF)
    square = jnp.sum(dot2(mine, gq[...]) * natural, axis=1, keepdims=True)
    inverse = lax.rsqrt(jnp.maximum(square, 0.0) * (1.0 / 4096.0) + 1e-6) * SCALE
    for head in range(4):
        q_s[head] = (dot2(mine, m[head]) * inverse).astype(BF)

    for head in range(4):
        qf = q_s[head].astype(F32)
        bound = jnp.sqrt(jnp.sum(qf * qf, axis=1, keepdims=True) * biggest)
        bound_s[head] = jnp.broadcast_to(bound, (4 * TOK, HD))
    acc_s[...] = jnp.zeros_like(acc_s)

    def step(j, carry):
        keys = pl.ds(pl.multiple_of(j * BLOCK, BLOCK), BLOCK)
        for head in range(4):
            scores = dot_nt(q_s[head], key_s[keys, :])
            weights = jnp.exp2(scores - bound_s[head, :, 0:1]).astype(BF)
            acc_s[head] += dot(weights, val_s[keys, :])
        return carry

    lax.fori_loop(0, KEYS // BLOCK, step, 0, unroll=2)

    @pl.when(jnp.logical_not(jnp.min(acc_s[:, :, HD:]) > TINY))
    def _():
        def careful_head(head, carry):
            acc_s[head] = jnp.zeros((4 * TOK, 2 * HD), F32)
            bound_s[head] = jnp.full((4 * TOK, HD), -1e30, F32)

            def careful(j, carry):
                keys = pl.ds(pl.multiple_of(j * 512, 512), 512)
                scores = dot_nt(q_s[head], key_s[keys, :])
                before = bound_s[head, :, 0:1]
                top = jnp.maximum(before, jnp.max(scores, axis=1, keepdims=True))
                weights = jnp.exp2(scores - top).astype(BF)
                acc_s[head] = acc_s[head] * jnp.exp2(before - top) + dot(weights, val_s[keys, :])
                bound_s[head] = jnp.broadcast_to(top, (4 * TOK, HD))
                return carry

            return lax.fori_loop(0, KEYS // 512, careful, carry)

        lax.fori_loop(0, 4, careful_head, 0)

    for head in range(4):
        mixed = (acc_s[head, :, :HD] / acc_s[head, :, HD:]).astype(BF)
        columns = slice(head * HD, (head + 1) * HD)
        attn_out[:, columns] = dot(mixed, wv[:, columns]).astype(BF)


def hi_attention(pos, lats, early, conv, b1, second, b2, gq, gk, m, value_weight):
    args = (*lats, *early, conv, b1, second, b2, gq, gk, m, value_weight)
    in_specs = [whole(a.shape) for a in args]
    in_specs[-1] = pl.BlockSpec((HD, 4 * HD), lambda i, pos: (0, pos[3]))
    return pl.pallas_call(
        hi_kernel,
        grid_spec=pltpu.PrefetchScalarGridSpec(
            num_scalar_prefetch=1,
            grid=(1,),
            in_specs=in_specs,
            out_specs=[whole((4 * TOK, 4 * HD)), whole((2 * W_LO, HD))],
            scratch_shapes=[
                pltpu.VMEM((3, FRAMES + 2, H_LO + 2, W_LO, HD), BF),
                pltpu.VMEM((FRAMES, TOK, HD), BF),
                pltpu.VMEM((KEYS, HD), BF),
                pltpu.VMEM((KEYS, 2 * HD), BF),
                pltpu.VMEM((4, 4 * TOK, HD), BF),
                pltpu.VMEM((4 * TOK, HD), F32),
                pltpu.VMEM((4, 4 * TOK, 2 * HD), F32),
                pltpu.VMEM((4, 4 * TOK, HD), F32),
            ],
        ),
        out_shape=[
            jax.ShapeDtypeStruct((4 * TOK, 4 * HD), BF),
            jax.ShapeDtypeStruct((2 * W_LO, HD), BF),
        ],
        compiler_params=pltpu.CompilerParams(vmem_limit_bytes=LARGE),
        name="hi",
    )(pos, *args)


def z_shift(step):
    return [(i, (i & 9) | ((((i >> 1) + step) & 3) << 1)) for i in range(16)]


def trade(value, partner):
    pairs = []
    for seq in range(16):
        for head in range(8):
            x, y, z, core = (seq >> 3) * 2 + (head & 1), head >> 1, (seq >> 1) & 3, seq & 1
            x, y, z, core = partner(x, y, z, core)
            other = ((x >> 1) * 8 + z * 2 + core) * 8 + y * 2 + (x & 1)
            pairs.append((seq * 8 + head, other))
    return lax.ppermute(value, ("seq", "head"), pairs)


def to_core(x, y, z, core):
    return x, y, z, core ^ 1


def to_x_far(x, y, z, core):
    return x ^ 2, y, z, core


def to_x_near(x, y, z, core):
    return x ^ 3, y, z, core


ROUNDS = ((("x", "x"), (1,)), (("y", "z"), (1, 3, 2)), (("z", "y"), (1, 3, 2)))


def along(axes, bit):
    def partner(x, y, z, core):
        flip = {"x": 0, "y": 0, "z": 0, axes[core]: bit}
        return x ^ flip["x"], y ^ flip["y"], z ^ flip["z"], core

    return partner


def sum_round(value, axes, bits):
    arrived = [trade(value, along(axes, bit)).astype(F32) for bit in bits]
    return sum(arrived, value.astype(F32)).astype(BF)


def local(
    hidden_low,
    query_low,
    key_low,
    value_low,
    out_weight,
    latent_weight,
    conv_first,
    bias_first,
    conv_second,
    bias_second,
    query_weight,
    key_weight,
    value_weight,
    query_gain,
    key_gain,
):
    seq, head = lax.axis_index("seq"), lax.axis_index("head")
    pos = jnp.stack([seq // 8, (seq // 2) % 4, seq % 2, head]).astype(jnp.int32)
    pieces = pack(query_low, key_low, value_low)
    pieces = [pieces[0]] + [
        lax.ppermute(pieces[step], "seq", z_shift(step)) for step in (1, 2, 3)
    ]
    w2, hl, m, gq, gk = prep(
        pos, out_weight, latent_weight, hidden_low, query_weight, key_weight, query_gain, key_gain
    )
    kv = jnp.concatenate([piece[:, HD:] for piece in pieces], axis=0)
    kv_x = trade(kv, to_x_far)
    kv_c = trade(kv, to_core)
    kv_x, w2, hl, m, gq, gk = lax.optimization_barrier((kv_x, w2, hl, m, gq, gk))
    kv_xc = trade(kv_x, to_core)
    latent = low_attention(pos, pieces, (kv, kv_c, kv_x, kv_xc), w2, hl)
    for axes, bits in ROUNDS:
        latent = sum_round(latent, axes, bits)
    upsampler = (
        conv_first.reshape(27 * HD, -1),
        bias_first.reshape(1, -1),
        conv_second,
        bias_second.reshape(1, -1),
    )
    lat_x = trade(latent, to_x_near)
    lat_c = trade(latent, to_core)
    early = early_frames(pos, (latent, lat_c), *upsampler, gk)
    lat_x, *early = lax.optimization_barrier((lat_x, *early))
    lat_xc = trade(lat_x, to_core)
    attn, up = hi_attention(
        pos, (latent, lat_c, lat_x, lat_xc), early, *upsampler, gq, gk, m, value_weight
    )
    return attn, up


def solution(mesh):
    placed = (
        P("seq", None),
        P("seq", "head"),
        P("seq", "head"),
        P("seq", "head"),
        P("head", None),
    ) + (P(),) * 10
    return jax.shard_map(
        local,
        mesh=mesh,
        in_specs=placed,
        out_specs=(P("seq", "head"), P(("seq", "head"), None)),
        check_vma=False,
    )
```

```python
import functools
import math

import jax
import jax.numpy as jnp
from jax import lax
from jax.experimental import pallas as pl
from jax.experimental.pallas import tpu as pltpu
from jax.sharding import PartitionSpec as P

HD = 128
H_LO = 4
W_LO = 32
FRAMES = 16
TOK = H_LO * W_LO
KEYS = 4 * FRAMES * TOK
LOG2E = 1.4426950408889634
SCALE = LOG2E / math.sqrt(HD)
BF = jnp.bfloat16
F32 = jnp.float32
SMALL, LARGE = 16 * 2**20, 46 * 2**20
NT = (((1,), (1,)), ((), ()))


def dot(a, b):
    return jnp.dot(a, b, preferred_element_type=F32)


def dot_nt(a, b):
    return lax.dot_general(a, b, NT, preferred_element_type=F32)


def split2(x):
    high = x.astype(BF)
    low = (x - high.astype(F32)).astype(BF)
    return jnp.concatenate([high, low], axis=1)


def dot2(a, b2):
    both = dot(a, b2)
    half = both.shape[1] // 2
    return both[:, :half] + both[:, half:]


def whole(shape):
    return pl.BlockSpec(shape, lambda *_: (0,) * len(shape))


def pack_kernel(q_ref, k_ref, v_ref, *outs):
    z = (lax.axis_index("seq") >> 1) & 3
    for shift, out in enumerate(outs):
        head = (z + shift) & 3
        columns = pl.ds(pl.multiple_of(head * HD, HD), HD)
        out[:, 0:HD] = q_ref[:, columns]
        out[:, HD : 2 * HD] = k_ref[:, columns]
        out[:, 2 * HD : 3 * HD] = v_ref[:, columns]


def pack(q, k, v):
    return pl.pallas_call(
        pack_kernel,
        out_shape=[pltpu.VMEM((TOK, 3 * HD), BF)] * 4,
        compiler_params=pltpu.CompilerParams(vmem_limit_bytes=SMALL),
        name="pack",
    )(*(pltpu.with_memory_space_constraint(array, pltpu.HBM) for array in (q, k, v)))


def prep_kernel(pos, ow, lw, hid, wqh, wkh, gq, gk, wq, wk, w2_out, hl_out, m_out, gq_out, gk_out):
    del pos
    w2_out[...] = split2(dot(ow[...], lw[...]))
    hl_out[...] = dot(hid[...], lw[...])
    gain = gq[...] * gk[...]
    for head in range(4):
        cols = slice(head * HD, (head + 1) * HD)
        left = split2(wqh[:, cols].astype(F32) * gain[:, cols])
        right = wkh[:, cols]
        m_out[head] = split2(dot_nt(left[:, :HD], right) + dot_nt(left[:, HD:], right))
    gq_out[...] = split2(dot_nt(wq[...], wq[...]))
    gk_out[...] = split2(dot_nt(wk[...], wk[...]))


def prep(pos, out_weight, latent_weight, hidden, query_weight, key_weight, query_gain, key_gain):
    width = hidden.shape[1]
    share = TOK // 8
    group = 4 * HD
    return pl.pallas_call(
        prep_kernel,
        grid_spec=pltpu.PrefetchScalarGridSpec(
            num_scalar_prefetch=1,
            grid=(1,),
            in_specs=[
                pl.BlockSpec((HD, width), lambda i, pos: (pos[1], 0)),
                whole(latent_weight.shape),
                pl.BlockSpec((share, width), lambda i, pos: (pos[3], 0)),
                pl.BlockSpec((HD, group), lambda i, pos: (0, pos[3])),
                pl.BlockSpec((HD, group), lambda i, pos: (0, pos[3])),
                pl.BlockSpec((1, group), lambda i, pos: (0, pos[3])),
                pl.BlockSpec((1, group), lambda i, pos: (0, pos[3])),
                whole(query_weight.shape),
                whole(key_weight.shape),
            ],
            out_specs=[
                whole((HD, 2 * HD)),
                whole((share, HD)),
                whole((4, HD, 2 * HD)),
                whole((HD, 2 * HD)),
                whole((HD, 2 * HD)),
            ],
        ),
        out_shape=[
            jax.ShapeDtypeStruct((HD, 2 * HD), BF),
            jax.ShapeDtypeStruct((share, HD), F32),
            jax.ShapeDtypeStruct((4, HD, 2 * HD), BF),
            jax.ShapeDtypeStruct((HD, 2 * HD), BF),
            jax.ShapeDtypeStruct((HD, 2 * HD), BF),
        ],
        compiler_params=pltpu.CompilerParams(vmem_limit_bytes=SMALL),
        cost_estimate=pl.CostEstimate(flops=900_000_000, bytes_accessed=5_000_000, transcendentals=0),
        name="prep",
    )(
        pos,
        *(
            pltpu.with_memory_space_constraint(array, pltpu.HBM)
            for array in (
                out_weight,
                latent_weight,
                hidden,
                query_weight,
                key_weight,
                query_gain.reshape(1, -1),
                key_gain.reshape(1, -1),
                query_weight,
                key_weight,
            )
        ),
    )


def low_kernel(pos, p0, p1, p2, p3, kv0, kv1, kv2, kv3, w2, hl, out, q_s, part_s):
    z = pos[1]
    for shift, piece in enumerate((p0, p1, p2, p3)):
        q_s[lax.rem(z + 4 - shift, 4)] = piece[:, 0:HD]
    for half in range(2):
        q = q_s[2 * half : 2 * half + 2].reshape(2 * TOK, HD)
        blocks = (kv0, kv1, kv2, kv3)
        scores = [dot_nt(q, kv[:, 0:HD]) * SCALE for kv in blocks]
        top = functools.reduce(jnp.maximum, [jnp.max(s, axis=1, keepdims=True) for s in scores])
        total = jnp.zeros((2 * TOK, 1), F32)
        numerator = jnp.zeros((2 * TOK, HD), F32)
        for s, kv in zip(scores, blocks):
            e = jnp.exp2(s - top)
            total = total + jnp.sum(e, axis=1, keepdims=True)
            numerator = numerator + dot(e.astype(BF), kv[:, HD : 2 * HD])
        attn = (numerator / total).astype(BF)
        part_s[2 * half * TOK : (2 * half + 2) * TOK, :] = dot2(attn, w2[...])
    share = TOK // 8
    rows = pl.ds(pl.multiple_of(z * TOK + pos[3] * share, share), share)
    part_s[rows, :] = part_s[rows, :] + hl[...]
    out[...] = part_s[...].astype(BF)


def low_attention(pos, pieces, kvs, w2, hl):
    args = (*pieces, *kvs, w2, hl)
    return pl.pallas_call(
        low_kernel,
        grid_spec=pltpu.PrefetchScalarGridSpec(
            num_scalar_prefetch=1,
            grid=(1,),
            in_specs=[whole(a.shape) for a in args],
            out_specs=whole((4 * TOK, HD)),
            scratch_shapes=[pltpu.VMEM((4, TOK, HD), BF), pltpu.VMEM((4 * TOK, HD), F32)],
        ),
        out_shape=pltpu.VMEM((4 * TOK, HD), BF),
        compiler_params=pltpu.CompilerParams(vmem_limit_bytes=2 * SMALL),
        name="low",
    )(pos, *args)


PAIRS = FRAMES // 2
CHUNK = 4
TAPS = 9 * HD
BLOCK = 2048
TINY = 2.0**-90


def mids_kernel(conv, out):
    ends = conv[0:TAPS, :].astype(F32) + conv[2 * TAPS : 3 * TAPS, :].astype(F32)
    centre = conv[TAPS : 2 * TAPS, :].astype(F32)
    out[0:TAPS, :] = (0.5 * (ends + centre)).astype(BF)
    out[TAPS : 2 * TAPS, :] = (0.5 * (ends - centre)).astype(BF)


def middle_weights(conv):
    return pl.pallas_call(
        mids_kernel,
        out_shape=jax.ShapeDtypeStruct((2 * TAPS, conv.shape[1]), BF),
        compiler_params=pltpu.CompilerParams(vmem_limit_bytes=SMALL),
        cost_estimate=pl.CostEstimate(flops=3_000_000, bytes_accessed=6_000_000, transcendentals=0),
        name="mids",
    )(conv)


def hi_kernel(
    pos,
    lat0,
    lat1,
    lat2,
    lat3,
    conv,
    mids,
    b1,
    second,
    b2,
    gq,
    gk,
    m,
    wv,
    attn_out,
    up_out,
    grid_s,
    lat_s,
    key_s,
    val_s,
    q_s,
    nat_s,
    acc_s,
    bound_s,
    prod_s,
):
    x, z, c, g = pos[0], pos[1], pos[2], pos[3]
    for dx, dc, piece in ((0, 0, lat0), (0, 1, lat1), (1, 0, lat2), (1, 1, lat3)):
        px = lax.bitwise_xor(x, dx)
        pc = lax.bitwise_xor(c, dc)
        for pz in range(4):
            lat_s[1 + px * 8 + pz * 2 + pc] = piece[pz * TOK : (pz + 1) * TOK, :]
    lat_s[0:1] = jnp.zeros((1, TOK, HD), BF)
    lat_s[FRAMES + 1 : FRAMES + 2] = jnp.zeros((1, TOK, HD), BF)
    edge = jnp.zeros((12, PAIRS, 1, W_LO, HD), BF)
    grid_s[:, :, 0:1] = edge
    grid_s[:, :, H_LO + 1 : H_LO + 2] = edge
    d0, d1, d2, d3 = (
        jnp.concatenate([lat_s[2 * pair + d : 2 * pair + d + 1] for pair in range(PAIRS)], axis=0).astype(F32)
        for d in range(4)
    )
    count = PAIRS * TOK
    column = lax.broadcasted_iota(jnp.int32, (count, HD), 0) & (W_LO - 1)
    for index, mixed in enumerate((d0 - d2, d1 + d2, d2 - d1, d1 - d3)):
        mixed = mixed.reshape(count, HD)
        left = jnp.where(column == 0, 0.0, pltpu.roll(mixed, 1, 0))
        right = jnp.where(column == W_LO - 1, 0.0, pltpu.roll(mixed, count - 1, 0))
        for offset, shifted in enumerate((left, mixed, right)):
            grid_s[3 * index + offset, :, 1 : H_LO + 1] = shifted.astype(BF).reshape(PAIRS, H_LO, W_LO, HD)

    val_s[:, HD : 2 * HD] = jnp.ones((KEYS, HD), BF)
    biggest = jnp.zeros((1, 1), F32)
    rows = CHUNK * TOK
    weights = (conv.at[0:TAPS], mids.at[0:TAPS], mids.at[TAPS : 2 * TAPS], conv.at[2 * TAPS : 3 * TAPS])
    for first in range(0, PAIRS, CHUNK):
        def product(index):
            taps = []
            for b in range(3):
                for t in range(3):
                    taps.append(grid_s[3 * index + t, first : first + CHUNK, b : b + H_LO].reshape(rows, HD))
            return dot(jnp.concatenate(taps, axis=1), weights[index][...])

        prod_s[0] = product(1)
        prod_s[1] = product(2)
        prod_s[2] = prod_s[0] - prod_s[1] - product(3)
        prod_s[0] = prod_s[0] + prod_s[1] + product(0)
        for parity in range(2):
            middle = prod_s[2 * parity] + b1[...]
            middle = (middle * (0.5 * jnp.tanh(0.5 * middle) + 0.5)).astype(BF)
            sub = dot(middle, second[...]) + b2[...]
            mine = [lat_s[1 + 2 * pair + parity] for pair in range(first, first + CHUNK)]
            base = jnp.concatenate(mine, axis=0).astype(F32)
            for s in range(4):
                up = (sub[:, s * HD : (s + 1) * HD] + base).astype(BF)
                upf = up.astype(F32)
                square = jnp.sum(dot2(up, gk[...]) * upf, axis=1, keepdims=True)
                inverse = lax.rsqrt(jnp.maximum(square, 0.0) * (1.0 / 4096.0) + 1e-6)
                key = (upf * inverse).astype(BF)
                where = pl.ds(s * FRAMES * TOK + 2 * first * TOK + parity * rows, rows)
                val_s[where, 0:HD] = up
                key_s[where, :] = key
                keyf = key.astype(F32)
                length = jnp.sum(keyf * keyf, axis=1, keepdims=True)
                biggest = jnp.maximum(biggest, jnp.max(length, axis=0, keepdims=True))

    place = x * (2 * CHUNK) + c * CHUNK + z
    own = jnp.concatenate(
        [val_s[pl.ds(pl.multiple_of(s * FRAMES * TOK + place * TOK, TOK), TOK), 0:HD] for s in range(4)], axis=0
    )
    to = lax.broadcasted_iota(jnp.int32, (4 * TOK, 4 * TOK), 0)
    source = lax.broadcasted_iota(jnp.int32, (4 * TOK, 4 * TOK), 1)
    p, r = (to >> 6) & 1, to & 1
    wanted = (((p << 1) | r) << 7) | ((to >> 7) << 5) | ((to >> 1) & (W_LO - 1))
    natural = dot(jnp.where(source == wanted, 1.0, 0.0).astype(BF), own)
    nat_s[...] = natural
    up_out[...] = nat_s[pl.ds(pl.multiple_of(g * 2 * W_LO, 2 * W_LO), 2 * W_LO), :].astype(BF)
    mine = natural.astype(BF)
    square = jnp.sum(dot2(mine, gq[...]) * natural, axis=1, keepdims=True)
    inverse = lax.rsqrt(jnp.maximum(square, 0.0) * (1.0 / 4096.0) + 1e-6) * SCALE
    for head in range(4):
        q_s[head] = (dot2(mine, m[head]) * inverse).astype(BF)

    for head in range(4):
        qf = q_s[head].astype(F32)
        bound = jnp.sqrt(jnp.sum(qf * qf, axis=1, keepdims=True) * biggest)
        bound_s[head] = jnp.broadcast_to(bound, (4 * TOK, HD))
    acc_s[...] = jnp.zeros_like(acc_s)

    def step(j, carry):
        keys = pl.ds(pl.multiple_of(j * BLOCK, BLOCK), BLOCK)
        for head in range(4):
            scores = dot_nt(q_s[head], key_s[keys, :])
            weights = jnp.exp2(scores - bound_s[head, :, 0:1]).astype(BF)
            acc_s[head] += dot(weights, val_s[keys, :])
        return carry

    lax.fori_loop(0, KEYS // BLOCK, step, 0, unroll=2)

    @pl.when(jnp.logical_not(jnp.min(acc_s[:, :, HD:]) > TINY))
    def _():
        def careful_head(head, carry):
            acc_s[head] = jnp.zeros((4 * TOK, 2 * HD), F32)
            bound_s[head] = jnp.full((4 * TOK, HD), -1e30, F32)

            def careful(j, carry):
                keys = pl.ds(pl.multiple_of(j * 512, 512), 512)
                scores = dot_nt(q_s[head], key_s[keys, :])
                before = bound_s[head, :, 0:1]
                top = jnp.maximum(before, jnp.max(scores, axis=1, keepdims=True))
                weights = jnp.exp2(scores - top).astype(BF)
                acc_s[head] = acc_s[head] * jnp.exp2(before - top) + dot(weights, val_s[keys, :])
                bound_s[head] = jnp.broadcast_to(top, (4 * TOK, HD))
                return carry

            return lax.fori_loop(0, KEYS // 512, careful, carry)

        lax.fori_loop(0, 4, careful_head, 0)

    for head in range(4):
        mixed = (acc_s[head, :, :HD] / acc_s[head, :, HD:]).astype(BF)
        columns = slice(head * HD, (head + 1) * HD)
        attn_out[:, columns] = dot(mixed, wv[:, columns]).astype(BF)


def hi_attention(pos, lats, conv, mids, bias_first, conv_second, bias_second, gq, gk, m, value_weight):
    args = (*lats, conv, mids, bias_first.reshape(1, -1), conv_second, bias_second.reshape(1, -1), gq, gk, m, value_weight)
    in_specs = [whole(a.shape) for a in args]
    in_specs[-1] = pl.BlockSpec((HD, 4 * HD), lambda i, pos: (0, pos[3]))
    return pl.pallas_call(
        hi_kernel,
        grid_spec=pltpu.PrefetchScalarGridSpec(
            num_scalar_prefetch=1,
            grid=(1,),
            in_specs=in_specs,
            out_specs=[whole((4 * TOK, 4 * HD)), whole((2 * W_LO, HD))],
            scratch_shapes=[
                pltpu.VMEM((12, PAIRS, H_LO + 2, W_LO, HD), BF),
                pltpu.VMEM((FRAMES + 2, TOK, HD), BF),
                pltpu.VMEM((KEYS, HD), BF),
                pltpu.VMEM((KEYS, 2 * HD), BF),
                pltpu.VMEM((4, 4 * TOK, HD), BF),
                pltpu.VMEM((4 * TOK, HD), F32),
                pltpu.VMEM((4, 4 * TOK, 2 * HD), F32),
                pltpu.VMEM((4, 4 * TOK, HD), F32),
                pltpu.VMEM((3, CHUNK * TOK, conv.shape[1]), F32),
            ],
        ),
        out_shape=[
            jax.ShapeDtypeStruct((4 * TOK, 4 * HD), BF),
            jax.ShapeDtypeStruct((2 * W_LO, HD), BF),
        ],
        compiler_params=pltpu.CompilerParams(vmem_limit_bytes=LARGE),
        name="hi",
    )(pos, *args)


def z_shift(step):
    return [(i, (i & 9) | ((((i >> 1) + step) & 3) << 1)) for i in range(16)]


def trade(value, partner):
    pairs = []
    for seq in range(16):
        for head in range(8):
            x, y, z, core = (seq >> 3) * 2 + (head & 1), head >> 1, (seq >> 1) & 3, seq & 1
            x, y, z, core = partner(x, y, z, core)
            other = ((x >> 1) * 8 + z * 2 + core) * 8 + y * 2 + (x & 1)
            pairs.append((seq * 8 + head, other))
    return lax.ppermute(value, ("seq", "head"), pairs)


def to_core(x, y, z, core):
    return x, y, z, core ^ 1


def to_x_far(x, y, z, core):
    return x ^ 2, y, z, core


def to_x_near(x, y, z, core):
    return x ^ 3, y, z, core


ROUNDS = (("yz", (1, 3, 2)), ("zy", (1, 3, 2)))


def along(axes, bit):
    def partner(x, y, z, core):
        flip = {"x": 0, "y": 0, "z": 0, axes[core]: bit}
        return x ^ flip["x"], y ^ flip["y"], z ^ flip["z"], core

    return partner


def sum_round(value, axes, bits):
    return add_up(value, [trade(value, along(axes, bit)) for bit in bits])


def add_up(value, arrived):
    return sum((other.astype(F32) for other in arrived), value.astype(F32)).astype(BF)


def local(
    hidden_low,
    query_low,
    key_low,
    value_low,
    out_weight,
    latent_weight,
    conv_first,
    bias_first,
    conv_second,
    bias_second,
    query_weight,
    key_weight,
    value_weight,
    query_gain,
    key_gain,
):
    seq, head = lax.axis_index("seq"), lax.axis_index("head")
    pos = jnp.stack([seq // 8, (seq // 2) % 4, seq % 2, head]).astype(jnp.int32)
    pieces = pack(query_low, key_low, value_low)
    pieces = [pieces[0]] + [
        lax.ppermute(pieces[step], "seq", z_shift(step)) for step in (1, 2, 3)
    ]
    w2, hl, m, gq, gk = prep(
        pos, out_weight, latent_weight, hidden_low, query_weight, key_weight, query_gain, key_gain
    )
    kv = jnp.concatenate([piece[:, HD:] for piece in pieces], axis=0)
    kv_x = trade(kv, to_x_far)
    kv_c = trade(kv, to_core)
    kv_x, w2, hl, m, gq, gk = lax.optimization_barrier((kv_x, w2, hl, m, gq, gk))
    kv_xc = trade(kv_x, to_core)
    latent = low_attention(pos, pieces, (kv, kv_c, kv_x, kv_xc), w2, hl)
    conv = conv_first.reshape(27 * HD, -1)
    other, mids = lax.optimization_barrier((trade(latent, along("xx", 1)), middle_weights(conv)))
    latent = add_up(latent, [other])
    for axes, bits in ROUNDS:
        latent = sum_round(latent, axes, bits)
    lat_x = trade(latent, to_x_near)
    lat_c = trade(latent, to_core)
    lat_xc = trade(lat_x, to_core)
    attn, up = hi_attention(
        pos,
        (latent, lat_c, lat_x, lat_xc),
        conv,
        mids,
        bias_first,
        conv_second,
        bias_second,
        gq,
        gk,
        m,
        value_weight,
    )
    return attn, up


def solution(mesh):
    placed = (
        P("seq", None),
        P("seq", "head"),
        P("seq", "head"),
        P("seq", "head"),
        P("head", None),
    ) + (P(),) * 10
    return jax.shard_map(
        local,
        mesh=mesh,
        in_specs=placed,
        out_specs=(P("seq", "head"), P(("seq", "head"), None)),
        check_vma=False,
    )
```

```python
import functools
import math

import jax
import jax.numpy as jnp
from jax import lax
from jax.experimental import pallas as pl
from jax.experimental.pallas import tpu as pltpu
from jax.sharding import PartitionSpec as P

HD = 128
H_LO = 4
W_LO = 32
FRAMES = 16
TOK = H_LO * W_LO
KEYS = 4 * FRAMES * TOK
LOG2E = 1.4426950408889634
SCALE = LOG2E / math.sqrt(HD)
BF = jnp.bfloat16
F32 = jnp.float32
SMALL, LARGE = 16 * 2**20, 46 * 2**20
NT = (((1,), (1,)), ((), ()))


def dot(a, b):
    return jnp.dot(a, b, preferred_element_type=F32)


def dot_nt(a, b):
    return lax.dot_general(a, b, NT, preferred_element_type=F32)


def split2(x):
    high = x.astype(BF)
    low = (x - high.astype(F32)).astype(BF)
    return jnp.concatenate([high, low], axis=1)


def dot2(a, b2):
    both = dot(a, b2)
    half = both.shape[1] // 2
    return both[:, :half] + both[:, half:]


def whole(shape):
    return pl.BlockSpec(shape, lambda *_: (0,) * len(shape))


def pack_kernel(q_ref, k_ref, v_ref, *outs):
    z = (lax.axis_index("seq") >> 1) & 3
    for shift, out in enumerate(outs):
        head = z ^ shift
        columns = pl.ds(pl.multiple_of(head * HD, HD), HD)
        out[:, 0:HD] = q_ref[:, columns]
        out[:, HD : 2 * HD] = k_ref[:, columns]
        out[:, 2 * HD : 3 * HD] = v_ref[:, columns]


def pack(q, k, v):
    return pl.pallas_call(
        pack_kernel,
        out_shape=[pltpu.VMEM((TOK, 3 * HD), BF)] * 4,
        compiler_params=pltpu.CompilerParams(vmem_limit_bytes=SMALL),
        name="pack",
    )(*(pltpu.with_memory_space_constraint(array, pltpu.HBM) for array in (q, k, v)))


def prep_kernel(pos, ow, lw, hid, wqh, wkh, gq, gk, wq, wk, w2_out, hl_out, m_out, gq_out, gk_out):
    del pos
    w2_out[...] = split2(dot(ow[...], lw[...]))
    hl_out[...] = dot(hid[...], lw[...])
    gain = gq[...] * gk[...]
    for head in range(4):
        cols = slice(head * HD, (head + 1) * HD)
        left = split2(wqh[:, cols].astype(F32) * gain[:, cols])
        right = wkh[:, cols]
        m_out[head] = split2(dot_nt(left[:, :HD], right) + dot_nt(left[:, HD:], right))
    gq_out[...] = split2(dot_nt(wq[...], wq[...]))
    gk_out[...] = split2(dot_nt(wk[...], wk[...]))


def prep(pos, out_weight, latent_weight, hidden, query_weight, key_weight, query_gain, key_gain):
    width = hidden.shape[1]
    share = TOK // 8
    group = 4 * HD
    return pl.pallas_call(
        prep_kernel,
        grid_spec=pltpu.PrefetchScalarGridSpec(
            num_scalar_prefetch=1,
            grid=(1,),
            in_specs=[
                pl.BlockSpec((HD, width), lambda i, pos: (pos[1], 0)),
                whole(latent_weight.shape),
                pl.BlockSpec((share, width), lambda i, pos: (pos[3], 0)),
                pl.BlockSpec((HD, group), lambda i, pos: (0, pos[3])),
                pl.BlockSpec((HD, group), lambda i, pos: (0, pos[3])),
                pl.BlockSpec((1, group), lambda i, pos: (0, pos[3])),
                pl.BlockSpec((1, group), lambda i, pos: (0, pos[3])),
                whole(query_weight.shape),
                whole(key_weight.shape),
            ],
            out_specs=[
                whole((HD, 2 * HD)),
                whole((share, HD)),
                whole((4, HD, 2 * HD)),
                whole((HD, 2 * HD)),
                whole((HD, 2 * HD)),
            ],
        ),
        out_shape=[
            jax.ShapeDtypeStruct((HD, 2 * HD), BF),
            jax.ShapeDtypeStruct((share, HD), F32),
            jax.ShapeDtypeStruct((4, HD, 2 * HD), BF),
            jax.ShapeDtypeStruct((HD, 2 * HD), BF),
            jax.ShapeDtypeStruct((HD, 2 * HD), BF),
        ],
        compiler_params=pltpu.CompilerParams(vmem_limit_bytes=SMALL),
        cost_estimate=pl.CostEstimate(flops=900_000_000, bytes_accessed=5_000_000, transcendentals=0),
        name="prep",
    )(
        pos,
        *(
            pltpu.with_memory_space_constraint(array, pltpu.HBM)
            for array in (
                out_weight,
                latent_weight,
                hidden,
                query_weight,
                key_weight,
                query_gain.reshape(1, -1),
                key_gain.reshape(1, -1),
                query_weight,
                key_weight,
            )
        ),
    )


def low_kernel(pos, p0, p1, p2, p3, kv0, kv1, kv2, kv3, w2, hl, out, q_s, part_s):
    z = pos[1]
    for shift, piece in enumerate((p0, p1, p2, p3)):
        q_s[lax.bitwise_xor(z, shift)] = piece[:, 0:HD]
    for half in range(2):
        q = q_s[2 * half : 2 * half + 2].reshape(2 * TOK, HD)
        blocks = (kv0, kv1, kv2, kv3)
        scores = [dot_nt(q, kv[:, 0:HD]) * SCALE for kv in blocks]
        top = functools.reduce(jnp.maximum, [jnp.max(s, axis=1, keepdims=True) for s in scores])
        total = jnp.zeros((2 * TOK, 1), F32)
        numerator = jnp.zeros((2 * TOK, HD), F32)
        for s, kv in zip(scores, blocks):
            e = jnp.exp2(s - top)
            total = total + jnp.sum(e, axis=1, keepdims=True)
            numerator = numerator + dot(e.astype(BF), kv[:, HD : 2 * HD])
        attn = (numerator / total).astype(BF)
        part_s[2 * half * TOK : (2 * half + 2) * TOK, :] = dot2(attn, w2[...])
    share = TOK // 8
    rows = pl.ds(pl.multiple_of(z * TOK + pos[3] * share, share), share)
    part_s[rows, :] = part_s[rows, :] + hl[...]
    out[...] = part_s[...].astype(BF)


def low_attention(pos, pieces, kvs, w2, hl):
    args = (*pieces, *kvs, w2, hl)
    return pl.pallas_call(
        low_kernel,
        grid_spec=pltpu.PrefetchScalarGridSpec(
            num_scalar_prefetch=1,
            grid=(1,),
            in_specs=[whole(a.shape) for a in args],
            out_specs=whole((4 * TOK, HD)),
            scratch_shapes=[pltpu.VMEM((4, TOK, HD), BF), pltpu.VMEM((4 * TOK, HD), F32)],
        ),
        out_shape=pltpu.VMEM((4 * TOK, HD), BF),
        compiler_params=pltpu.CompilerParams(vmem_limit_bytes=2 * SMALL),
        name="low",
    )(pos, *args)


CHUNK = 4
BLOCK = 2048
TINY = 2.0**-90


def hi_kernel(
    pos,
    lat0,
    lat1,
    lat2,
    lat3,
    conv,
    b1,
    second,
    b2,
    gq,
    gk,
    m,
    wv,
    attn_out,
    up_out,
    grid_s,
    lat_s,
    key_s,
    val_s,
    q_s,
    nat_s,
    acc_s,
    bound_s,
):
    x, z, c, g = pos[0], pos[1], pos[2], pos[3]
    for dx, dc, piece in ((0, 0, lat0), (0, 1, lat1), (1, 0, lat2), (1, 1, lat3)):
        px = lax.bitwise_xor(x, dx)
        pc = lax.bitwise_xor(c, dc)
        for pz in range(4):
            lat_s[px * 8 + pz * 2 + pc] = piece[pz * TOK : (pz + 1) * TOK, :]
    edge = jnp.zeros((3, 1, H_LO + 2, W_LO, HD), BF)
    grid_s[:, 0:1] = edge
    grid_s[:, FRAMES + 1 : FRAMES + 2] = edge
    edge = jnp.zeros((3, FRAMES + 2, 1, W_LO, HD), BF)
    grid_s[:, :, 0:1] = edge
    grid_s[:, :, H_LO + 1 : H_LO + 2] = edge
    lat = lat_s[...].reshape(FRAMES * TOK, HD).astype(F32)
    column = lax.rem(lax.broadcasted_iota(jnp.int32, (FRAMES * TOK, HD), 0), W_LO)
    left = jnp.where(column == 0, 0.0, pltpu.roll(lat, 1, 0))
    right = jnp.where(column == W_LO - 1, 0.0, pltpu.roll(lat, FRAMES * TOK - 1, 0))
    for index, shifted in enumerate((left, lat, right)):
        grid_s[index, 1 : FRAMES + 1, 1 : H_LO + 1] = shifted.astype(BF).reshape(FRAMES, H_LO, W_LO, HD)

    val_s[:, HD : 2 * HD] = jnp.ones((KEYS, HD), BF)
    biggest = jnp.zeros((1, 1), F32)
    rows = CHUNK * TOK
    for first in range(0, FRAMES, CHUNK):
        taps = []
        for a in range(3):
            for b in range(3):
                for t in range(3):
                    taps.append(grid_s[t, first + a : first + a + CHUNK, b : b + H_LO].reshape(rows, HD))
        middle = dot(jnp.concatenate(taps, axis=1), conv[...]) + b1[...]
        middle = (middle * (0.5 * jnp.tanh(0.5 * middle) + 0.5)).astype(BF)
        sub = dot(middle, second[...]) + b2[...]
        base = lat_s[first : first + CHUNK].reshape(rows, HD).astype(F32)
        for s in range(4):
            up = (sub[:, s * HD : (s + 1) * HD] + base).astype(BF)
            upf = up.astype(F32)
            square = jnp.sum(dot2(up, gk[...]) * upf, axis=1, keepdims=True)
            inverse = lax.rsqrt(jnp.maximum(square, 0.0) * (1.0 / 4096.0) + 1e-6)
            key = (upf * inverse).astype(BF)
            where = pl.ds(s * FRAMES * TOK + first * TOK, rows)
            val_s[where, 0:HD] = up
            key_s[where, :] = key
            keyf = key.astype(F32)
            length = jnp.sum(keyf * keyf, axis=1, keepdims=True)
            biggest = jnp.maximum(biggest, jnp.max(length, axis=0, keepdims=True))

    frame = x * 8 + z * 2 + c
    own = jnp.concatenate(
        [val_s[pl.ds(pl.multiple_of(s * FRAMES * TOK + frame * TOK, TOK), TOK), 0:HD] for s in range(4)], axis=0
    )
    to = lax.broadcasted_iota(jnp.int32, (4 * TOK, 4 * TOK), 0)
    source = lax.broadcasted_iota(jnp.int32, (4 * TOK, 4 * TOK), 1)
    p, r = (to >> 6) & 1, to & 1
    wanted = (((p << 1) | r) << 7) | ((to >> 7) << 5) | ((to >> 1) & (W_LO - 1))
    natural = dot(jnp.where(source == wanted, 1.0, 0.0).astype(BF), own)
    nat_s[...] = natural
    up_out[...] = nat_s[pl.ds(pl.multiple_of(g * 2 * W_LO, 2 * W_LO), 2 * W_LO), :].astype(BF)
    mine = natural.astype(BF)
    square = jnp.sum(dot2(mine, gq[...]) * natural, axis=1, keepdims=True)
    inverse = lax.rsqrt(jnp.maximum(square, 0.0) * (1.0 / 4096.0) + 1e-6) * SCALE
    for head in range(4):
        q_s[head] = (dot2(mine, m[head]) * inverse).astype(BF)

    for head in range(4):
        qf = q_s[head].astype(F32)
        bound = jnp.sqrt(jnp.sum(qf * qf, axis=1, keepdims=True) * biggest)
        bound_s[head] = jnp.broadcast_to(bound, (4 * TOK, HD))
    acc_s[...] = jnp.zeros_like(acc_s)

    def step(j, carry):
        keys = pl.ds(pl.multiple_of(j * BLOCK, BLOCK), BLOCK)
        for head in range(4):
            scores = dot_nt(q_s[head], key_s[keys, :])
            weights = jnp.exp2(scores - bound_s[head, :, 0:1]).astype(BF)
            acc_s[head] += dot(weights, val_s[keys, :])
        return carry

    lax.fori_loop(0, KEYS // BLOCK, step, 0, unroll=2)

    def finish():
        for head in range(4):
            mixed = (acc_s[head, :, :HD] / acc_s[head, :, HD:]).astype(BF)
            columns = slice(head * HD, (head + 1) * HD)
            attn_out[:, columns] = dot(mixed, wv[:, columns]).astype(BF)

    weakest = jnp.min(acc_s[:, :, HD:])
    finish()

    @pl.when(jnp.logical_not(weakest > TINY))
    def _():
        def careful_head(head, carry):
            acc_s[head] = jnp.zeros((4 * TOK, 2 * HD), F32)
            bound_s[head] = jnp.full((4 * TOK, HD), -1e30, F32)

            def careful(j, carry):
                keys = pl.ds(pl.multiple_of(j * 512, 512), 512)
                scores = dot_nt(q_s[head], key_s[keys, :])
                before = bound_s[head, :, 0:1]
                top = jnp.maximum(before, jnp.max(scores, axis=1, keepdims=True))
                weights = jnp.exp2(scores - top).astype(BF)
                acc_s[head] = acc_s[head] * jnp.exp2(before - top) + dot(weights, val_s[keys, :])
                bound_s[head] = jnp.broadcast_to(top, (4 * TOK, HD))
                return carry

            return lax.fori_loop(0, KEYS // 512, careful, carry)

        lax.fori_loop(0, 4, careful_head, 0)
        finish()


def hi_attention(pos, lats, conv_first, bias_first, conv_second, bias_second, gq, gk, m, value_weight):
    mid = conv_second.shape[0]
    conv = conv_first.reshape(27 * HD, mid)
    args = (*lats, conv, bias_first.reshape(1, -1), conv_second, bias_second.reshape(1, -1), gq, gk, m, value_weight)
    in_specs = [whole(a.shape) for a in args]
    in_specs[-1] = pl.BlockSpec((HD, 4 * HD), lambda i, pos: (0, pos[3]))
    return pl.pallas_call(
        hi_kernel,
        grid_spec=pltpu.PrefetchScalarGridSpec(
            num_scalar_prefetch=1,
            grid=(1,),
            in_specs=in_specs,
            out_specs=[whole((4 * TOK, 4 * HD)), whole((2 * W_LO, HD))],
            scratch_shapes=[
                pltpu.VMEM((3, FRAMES + 2, H_LO + 2, W_LO, HD), BF),
                pltpu.VMEM((FRAMES, TOK, HD), BF),
                pltpu.VMEM((KEYS, HD), BF),
                pltpu.VMEM((KEYS, 2 * HD), BF),
                pltpu.VMEM((4, 4 * TOK, HD), BF),
                pltpu.VMEM((4 * TOK, HD), F32),
                pltpu.VMEM((4, 4 * TOK, 2 * HD), F32),
                pltpu.VMEM((4, 4 * TOK, HD), F32),
            ],
        ),
        out_shape=[
            jax.ShapeDtypeStruct((4 * TOK, 4 * HD), BF),
            jax.ShapeDtypeStruct((2 * W_LO, HD), BF),
        ],
        compiler_params=pltpu.CompilerParams(vmem_limit_bytes=LARGE),
        name="hi",
    )(pos, *args)


def z_swap(bits):
    return [(i, i ^ (bits << 1)) for i in range(16)]


def trade(value, partner):
    pairs = []
    for seq in range(16):
        for head in range(8):
            x, y, z, core = (seq >> 3) * 2 + (head & 1), head >> 1, (seq >> 1) & 3, seq & 1
            x, y, z, core = partner(x, y, z, core)
            other = ((x >> 1) * 8 + z * 2 + core) * 8 + y * 2 + (x & 1)
            pairs.append((seq * 8 + head, other))
    return lax.ppermute(value, ("seq", "head"), pairs)


def to_core(x, y, z, core):
    return x, y, z, core ^ 1


def to_x_far(x, y, z, core):
    return x ^ 2, y, z, core


def to_x_near(x, y, z, core):
    return x ^ 3, y, z, core


ROUNDS = ((("x", "x"), (1,)), (("y", "z"), (1, 3, 2)), (("z", "y"), (1, 3, 2)))


def along(axes, bit):
    def partner(x, y, z, core):
        flip = {"x": 0, "y": 0, "z": 0, axes[core]: bit}
        return x ^ flip["x"], y ^ flip["y"], z ^ flip["z"], core

    return partner


def sum_round(value, axes, bits):
    arrived = [trade(value, along(axes, bit)).astype(F32) for bit in bits]
    return sum(arrived, value.astype(F32)).astype(BF)


def local(
    hidden_low,
    query_low,
    key_low,
    value_low,
    out_weight,
    latent_weight,
    conv_first,
    bias_first,
    conv_second,
    bias_second,
    query_weight,
    key_weight,
    value_weight,
    query_gain,
    key_gain,
):
    seq, head = lax.axis_index("seq"), lax.axis_index("head")
    pos = jnp.stack([seq // 8, (seq // 2) % 4, seq % 2, head]).astype(jnp.int32)
    pieces = pack(query_low, key_low, value_low)
    pieces = [pieces[0]] + [
        lax.ppermute(pieces[step], "seq", z_swap(step)) for step in (1, 2, 3)
    ]
    w2, hl, m, gq, gk = prep(
        pos, out_weight, latent_weight, hidden_low, query_weight, key_weight, query_gain, key_gain
    )
    kv = jnp.concatenate([piece[:, HD:] for piece in pieces], axis=0)
    kv_x = trade(kv, to_x_far)
    kv_c = trade(kv, to_core)
    kv_x, w2, hl, m, gq, gk = lax.optimization_barrier((kv_x, w2, hl, m, gq, gk))
    kv_xc = trade(kv_x, to_core)
    latent = low_attention(pos, pieces, (kv, kv_c, kv_x, kv_xc), w2, hl)
    for axes, bits in ROUNDS:
        latent = sum_round(latent, axes, bits)
    lat_x = trade(latent, to_x_near)
    lat_c = trade(latent, to_core)
    lat_xc = trade(lat_x, to_core)
    attn, up = hi_attention(
        pos,
        (latent, lat_c, lat_x, lat_xc),
        conv_first,
        bias_first,
        conv_second,
        bias_second,
        gq,
        gk,
        m,
        value_weight,
    )
    return attn, up


def solution(mesh):
    placed = (
        P("seq", None),
        P("seq", "head"),
        P("seq", "head"),
        P("seq", "head"),
        P("head", None),
    ) + (P(),) * 10
    return jax.shard_map(
        local,
        mesh=mesh,
        in_specs=placed,
        out_specs=(P("seq", "head"), P(("seq", "head"), None)),
        check_vma=False,
    )
```

```python
import functools
import math

import jax
import jax.numpy as jnp
from jax import lax
from jax.experimental import pallas as pl
from jax.experimental.pallas import tpu as pltpu
from jax.sharding import PartitionSpec as P

HD = 128
H_LO = 4
W_LO = 32
FRAMES = 16
TOK = H_LO * W_LO
KEYS = 4 * FRAMES * TOK
LOG2E = 1.4426950408889634
SCALE = LOG2E / math.sqrt(HD)
BF = jnp.bfloat16
F32 = jnp.float32
SMALL, LARGE = 16 * 2**20, 46 * 2**20
NT = (((1,), (1,)), ((), ()))


def dot(a, b):
    return jnp.dot(a, b, preferred_element_type=F32)


def dot_nt(a, b):
    return lax.dot_general(a, b, NT, preferred_element_type=F32)


def split2(x):
    high = x.astype(BF)
    low = (x - high.astype(F32)).astype(BF)
    return jnp.concatenate([high, low], axis=1)


def dot2(a, b2):
    both = dot(a, b2)
    half = both.shape[1] // 2
    return both[:, :half] + both[:, half:]


def whole(shape):
    return pl.BlockSpec(shape, lambda *_: (0,) * len(shape))


def pack_kernel(q_ref, k_ref, v_ref, *outs):
    z = (lax.axis_index("seq") >> 1) & 3
    for shift, out in enumerate(outs):
        head = (z + shift) & 3
        columns = pl.ds(pl.multiple_of(head * HD, HD), HD)
        out[:, 0:HD] = q_ref[:, columns]
        out[:, HD : 2 * HD] = k_ref[:, columns]
        out[:, 2 * HD : 3 * HD] = v_ref[:, columns]


def pack(q, k, v):
    return pl.pallas_call(
        pack_kernel,
        out_shape=[pltpu.VMEM((TOK, 3 * HD), BF)] * 4,
        compiler_params=pltpu.CompilerParams(vmem_limit_bytes=SMALL),
        name="pack",
    )(*(pltpu.with_memory_space_constraint(array, pltpu.HBM) for array in (q, k, v)))


def prep_kernel(pos, ow, lw, hid, wqh, wkh, gq, gk, wq, wk, w2_out, hl_out, m_out, gq_out, gk_out):
    del pos
    w2_out[...] = split2(dot(ow[...], lw[...]))
    hl_out[...] = dot(hid[...], lw[...])
    gain = gq[...] * gk[...]
    for head in range(4):
        cols = slice(head * HD, (head + 1) * HD)
        left = split2(wqh[:, cols].astype(F32) * gain[:, cols])
        right = wkh[:, cols]
        m_out[head] = split2(dot_nt(left[:, :HD], right) + dot_nt(left[:, HD:], right))
    gq_out[...] = split2(dot_nt(wq[...], wq[...]))
    gk_out[...] = split2(dot_nt(wk[...], wk[...]))


def prep(pos, out_weight, latent_weight, hidden, query_weight, key_weight, query_gain, key_gain):
    width = hidden.shape[1]
    share = TOK // 8
    group = 4 * HD
    return pl.pallas_call(
        prep_kernel,
        grid_spec=pltpu.PrefetchScalarGridSpec(
            num_scalar_prefetch=1,
            grid=(1,),
            in_specs=[
                pl.BlockSpec((HD, width), lambda i, pos: (pos[1], 0)),
                whole(latent_weight.shape),
                pl.BlockSpec((share, width), lambda i, pos: (pos[3], 0)),
                pl.BlockSpec((HD, group), lambda i, pos: (0, pos[3])),
                pl.BlockSpec((HD, group), lambda i, pos: (0, pos[3])),
                pl.BlockSpec((1, group), lambda i, pos: (0, pos[3])),
                pl.BlockSpec((1, group), lambda i, pos: (0, pos[3])),
                whole(query_weight.shape),
                whole(key_weight.shape),
            ],
            out_specs=[
                whole((HD, 2 * HD)),
                whole((share, HD)),
                whole((4, HD, 2 * HD)),
                whole((HD, 2 * HD)),
                whole((HD, 2 * HD)),
            ],
        ),
        out_shape=[
            jax.ShapeDtypeStruct((HD, 2 * HD), BF),
            jax.ShapeDtypeStruct((share, HD), F32),
            jax.ShapeDtypeStruct((4, HD, 2 * HD), BF),
            jax.ShapeDtypeStruct((HD, 2 * HD), BF),
            jax.ShapeDtypeStruct((HD, 2 * HD), BF),
        ],
        compiler_params=pltpu.CompilerParams(vmem_limit_bytes=SMALL),
        cost_estimate=pl.CostEstimate(flops=900_000_000, bytes_accessed=5_000_000, transcendentals=0),
        name="prep",
    )(
        pos,
        *(
            pltpu.with_memory_space_constraint(array, pltpu.HBM)
            for array in (
                out_weight,
                latent_weight,
                hidden,
                query_weight,
                key_weight,
                query_gain.reshape(1, -1),
                key_gain.reshape(1, -1),
                query_weight,
                key_weight,
            )
        ),
    )


def low_kernel(pos, p0, p1, p2, p3, kv0, kv1, kv2, kv3, w2, hl, out, q_s, part_s):
    z = pos[1]
    for shift, piece in enumerate((p0, p1, p2, p3)):
        q_s[lax.rem(z + 4 - shift, 4)] = piece[:, 0:HD]
    for half in range(2):
        q = q_s[2 * half : 2 * half + 2].reshape(2 * TOK, HD)
        blocks = (kv0, kv1, kv2, kv3)
        scores = [dot_nt(q, kv[:, 0:HD]) * SCALE for kv in blocks]
        top = functools.reduce(jnp.maximum, [jnp.max(s, axis=1, keepdims=True) for s in scores])
        total = jnp.zeros((2 * TOK, 1), F32)
        numerator = jnp.zeros((2 * TOK, HD), F32)
        for s, kv in zip(scores, blocks):
            e = jnp.exp2(s - top)
            total = total + jnp.sum(e, axis=1, keepdims=True)
            numerator = numerator + dot(e.astype(BF), kv[:, HD : 2 * HD])
        attn = (numerator / total).astype(BF)
        part_s[2 * half * TOK : (2 * half + 2) * TOK, :] = dot2(attn, w2[...])
    share = TOK // 8
    rows = pl.ds(pl.multiple_of(z * TOK + pos[3] * share, share), share)
    part_s[rows, :] = part_s[rows, :] + hl[...]
    out[...] = part_s[...].astype(BF)


def low_attention(pos, pieces, kvs, w2, hl):
    args = (*pieces, *kvs, w2, hl)
    return pl.pallas_call(
        low_kernel,
        grid_spec=pltpu.PrefetchScalarGridSpec(
            num_scalar_prefetch=1,
            grid=(1,),
            in_specs=[whole(a.shape) for a in args],
            out_specs=whole((4 * TOK, HD)),
            scratch_shapes=[pltpu.VMEM((4, TOK, HD), BF), pltpu.VMEM((4 * TOK, HD), F32)],
        ),
        out_shape=pltpu.VMEM((4 * TOK, HD), BF),
        compiler_params=pltpu.CompilerParams(vmem_limit_bytes=2 * SMALL),
        name="low",
    )(pos, *args)


CHUNK = 4
BLOCK = 2048
TINY = 2.0**-90


def hi_kernel(
    pos,
    lat0,
    lat1,
    lat2,
    lat3,
    conv,
    b1,
    second,
    b2,
    gq,
    gk,
    m,
    wv,
    attn_out,
    up_out,
    grid_s,
    lat_s,
    key_s,
    val_s,
    q_s,
    nat_s,
    acc_s,
    bound_s,
):
    x, z, c, g = pos[0], pos[1], pos[2], pos[3]
    for dx, dc, piece in ((0, 0, lat0), (0, 1, lat1), (1, 0, lat2), (1, 1, lat3)):
        px = lax.bitwise_xor(x, dx)
        pc = lax.bitwise_xor(c, dc)
        for pz in range(4):
            lat_s[px * 8 + pz * 2 + pc] = piece[pz * TOK : (pz + 1) * TOK, :]
    edge = jnp.zeros((3, 1, H_LO + 2, W_LO, HD), BF)
    grid_s[:, 0:1] = edge
    grid_s[:, FRAMES + 1 : FRAMES + 2] = edge
    edge = jnp.zeros((3, FRAMES + 2, 1, W_LO, HD), BF)
    grid_s[:, :, 0:1] = edge
    grid_s[:, :, H_LO + 1 : H_LO + 2] = edge
    lat = lat_s[...].reshape(FRAMES * TOK, HD).astype(F32)
    column = lax.rem(lax.broadcasted_iota(jnp.int32, (FRAMES * TOK, HD), 0), W_LO)
    left = jnp.where(column == 0, 0.0, pltpu.roll(lat, 1, 0))
    right = jnp.where(column == W_LO - 1, 0.0, pltpu.roll(lat, FRAMES * TOK - 1, 0))
    for index, shifted in enumerate((left, lat, right)):
        grid_s[index, 1 : FRAMES + 1, 1 : H_LO + 1] = shifted.astype(BF).reshape(FRAMES, H_LO, W_LO, HD)

    val_s[:, HD : 2 * HD] = jnp.ones((KEYS, HD), BF)
    biggest = jnp.zeros((1, 1), F32)
    rows = CHUNK * TOK
    for first in range(0, FRAMES, CHUNK):
        taps = []
        for a in range(3):
            for b in range(3):
                for t in range(3):
                    taps.append(grid_s[t, first + a : first + a + CHUNK, b : b + H_LO].reshape(rows, HD))
        middle = dot(jnp.concatenate(taps, axis=1), conv[...]) + b1[...]
        middle = (middle * (0.5 * jnp.tanh(0.5 * middle) + 0.5)).astype(BF)
        sub = dot(middle, second[...]) + b2[...]
        base = lat_s[first : first + CHUNK].reshape(rows, HD).astype(F32)
        for s in range(4):
            up = (sub[:, s * HD : (s + 1) * HD] + base).astype(BF)
            upf = up.astype(F32)
            square = jnp.sum(dot2(up, gk[...]) * upf, axis=1, keepdims=True)
            inverse = lax.rsqrt(jnp.maximum(square, 0.0) * (1.0 / 4096.0) + 1e-6)
            key = (upf * inverse).astype(BF)
            where = pl.ds(s * FRAMES * TOK + first * TOK, rows)
            val_s[where, 0:HD] = up
            key_s[where, :] = key
            keyf = key.astype(F32)
            length = jnp.sum(keyf * keyf, axis=1, keepdims=True)
            biggest = jnp.maximum(biggest, jnp.max(length, axis=0, keepdims=True))

    frame = x * 8 + z * 2 + c
    own = jnp.concatenate(
        [val_s[pl.ds(pl.multiple_of(s * FRAMES * TOK + frame * TOK, TOK), TOK), 0:HD] for s in range(4)], axis=0
    )
    to = lax.broadcasted_iota(jnp.int32, (4 * TOK, 4 * TOK), 0)
    source = lax.broadcasted_iota(jnp.int32, (4 * TOK, 4 * TOK), 1)
    p, r = (to >> 6) & 1, to & 1
    wanted = (((p << 1) | r) << 7) | ((to >> 7) << 5) | ((to >> 1) & (W_LO - 1))
    natural = dot(jnp.where(source == wanted, 1.0, 0.0).astype(BF), own)
    nat_s[...] = natural
    up_out[...] = nat_s[pl.ds(pl.multiple_of(g * 2 * W_LO, 2 * W_LO), 2 * W_LO), :].astype(BF)
    mine = natural.astype(BF)
    square = jnp.sum(dot2(mine, gq[...]) * natural, axis=1, keepdims=True)
    inverse = lax.rsqrt(jnp.maximum(square, 0.0) * (1.0 / 4096.0) + 1e-6) * SCALE
    for head in range(4):
        q_s[head] = (dot2(mine, m[head]) * inverse).astype(BF)

    for head in range(4):
        qf = q_s[head].astype(F32)
        bound = jnp.sqrt(jnp.sum(qf * qf, axis=1, keepdims=True) * biggest)
        bound_s[head] = jnp.broadcast_to(bound, (4 * TOK, HD))
    acc_s[...] = jnp.zeros_like(acc_s)

    def step(j, carry):
        keys = pl.ds(pl.multiple_of(j * BLOCK, BLOCK), BLOCK)
        for head in range(4):
            scores = dot_nt(q_s[head], key_s[keys, :])
            weights = jnp.exp2(scores - bound_s[head, :, 0:1]).astype(BF)
            acc_s[head] += dot(weights, val_s[keys, :])
        return carry

    lax.fori_loop(0, KEYS // BLOCK, step, 0, unroll=2)

    def finish():
        for head in range(4):
            mixed = (acc_s[head, :, :HD] / acc_s[head, :, HD:]).astype(BF)
            columns = slice(head * HD, (head + 1) * HD)
            attn_out[:, columns] = dot(mixed, wv[:, columns]).astype(BF)

    weakest = jnp.min(acc_s[:, :, HD:])
    finish()

    @pl.when(jnp.logical_not(weakest > TINY))
    def _():
        def careful_head(head, carry):
            acc_s[head] = jnp.zeros((4 * TOK, 2 * HD), F32)
            bound_s[head] = jnp.full((4 * TOK, HD), -1e30, F32)

            def careful(j, carry):
                keys = pl.ds(pl.multiple_of(j * 512, 512), 512)
                scores = dot_nt(q_s[head], key_s[keys, :])
                before = bound_s[head, :, 0:1]
                top = jnp.maximum(before, jnp.max(scores, axis=1, keepdims=True))
                weights = jnp.exp2(scores - top).astype(BF)
                acc_s[head] = acc_s[head] * jnp.exp2(before - top) + dot(weights, val_s[keys, :])
                bound_s[head] = jnp.broadcast_to(top, (4 * TOK, HD))
                return carry

            return lax.fori_loop(0, KEYS // 512, careful, carry)

        lax.fori_loop(0, 4, careful_head, 0)
        finish()


def hi_attention(pos, lats, conv_first, bias_first, conv_second, bias_second, gq, gk, m, value_weight):
    mid = conv_second.shape[0]
    conv = conv_first.reshape(27 * HD, mid)
    args = (*lats, conv, bias_first.reshape(1, -1), conv_second, bias_second.reshape(1, -1), gq, gk, m, value_weight)
    in_specs = [whole(a.shape) for a in args]
    in_specs[-1] = pl.BlockSpec((HD, 4 * HD), lambda i, pos: (0, pos[3]))
    return pl.pallas_call(
        hi_kernel,
        grid_spec=pltpu.PrefetchScalarGridSpec(
            num_scalar_prefetch=1,
            grid=(1,),
            in_specs=in_specs,
            out_specs=[whole((4 * TOK, 4 * HD)), whole((2 * W_LO, HD))],
            scratch_shapes=[
                pltpu.VMEM((3, FRAMES + 2, H_LO + 2, W_LO, HD), BF),
                pltpu.VMEM((FRAMES, TOK, HD), BF),
                pltpu.VMEM((KEYS, HD), BF),
                pltpu.VMEM((KEYS, 2 * HD), BF),
                pltpu.VMEM((4, 4 * TOK, HD), BF),
                pltpu.VMEM((4 * TOK, HD), F32),
                pltpu.VMEM((4, 4 * TOK, 2 * HD), F32),
                pltpu.VMEM((4, 4 * TOK, HD), F32),
            ],
        ),
        out_shape=[
            jax.ShapeDtypeStruct((4 * TOK, 4 * HD), BF),
            jax.ShapeDtypeStruct((2 * W_LO, HD), BF),
        ],
        compiler_params=pltpu.CompilerParams(vmem_limit_bytes=LARGE),
        name="hi",
    )(pos, *args)


def z_shift(step):
    return [(i, (i & 9) | ((((i >> 1) + step) & 3) << 1)) for i in range(16)]


def trade(value, partner):
    pairs = []
    for seq in range(16):
        for head in range(8):
            x, y, z, core = (seq >> 3) * 2 + (head & 1), head >> 1, (seq >> 1) & 3, seq & 1
            x, y, z, core = partner(x, y, z, core)
            other = ((x >> 1) * 8 + z * 2 + core) * 8 + y * 2 + (x & 1)
            pairs.append((seq * 8 + head, other))
    return lax.ppermute(value, ("seq", "head"), pairs)


def to_core(x, y, z, core):
    return x, y, z, core ^ 1


def to_x_far(x, y, z, core):
    return x ^ 2, y, z, core


def to_x_near(x, y, z, core):
    return x ^ 3, y, z, core


ROUNDS = ((("x", "x"), (1,)), (("y", "z"), (1, 3, 2)), (("z", "y"), (1, 3, 2)))


def along(axes, bit):
    def partner(x, y, z, core):
        flip = {"x": 0, "y": 0, "z": 0, axes[core]: bit}
        return x ^ flip["x"], y ^ flip["y"], z ^ flip["z"], core

    return partner


def sum_round(value, axes, bits):
    arrived = [trade(value, along(axes, bit)).astype(F32) for bit in bits]
    return sum(arrived, value.astype(F32)).astype(BF)


def local(
    hidden_low,
    query_low,
    key_low,
    value_low,
    out_weight,
    latent_weight,
    conv_first,
    bias_first,
    conv_second,
    bias_second,
    query_weight,
    key_weight,
    value_weight,
    query_gain,
    key_gain,
):
    seq, head = lax.axis_index("seq"), lax.axis_index("head")
    pos = jnp.stack([seq // 8, (seq // 2) % 4, seq % 2, head]).astype(jnp.int32)
    pieces = pack(query_low, key_low, value_low)
    pieces = [pieces[0]] + [
        lax.ppermute(pieces[step], "seq", z_shift(step)) for step in (1, 2, 3)
    ]
    w2, hl, m, gq, gk = prep(
        pos, out_weight, latent_weight, hidden_low, query_weight, key_weight, query_gain, key_gain
    )
    kv = jnp.concatenate([piece[:, HD:] for piece in pieces], axis=0)
    kv_x = trade(kv, to_x_far)
    kv_c = trade(kv, to_core)
    kv_x, w2, hl, m, gq, gk = lax.optimization_barrier((kv_x, w2, hl, m, gq, gk))
    kv_xc = trade(kv_x, to_core)
    latent = low_attention(pos, pieces, (kv, kv_c, kv_x, kv_xc), w2, hl)
    for axes, bits in ROUNDS:
        latent = sum_round(latent, axes, bits)
    lat_x = trade(latent, to_x_near)
    lat_c = trade(latent, to_core)
    lat_xc = trade(lat_x, to_core)
    attn, up = hi_attention(
        pos,
        (latent, lat_c, lat_x, lat_xc),
        conv_first,
        bias_first,
        conv_second,
        bias_second,
        gq,
        gk,
        m,
        value_weight,
    )
    return attn, up


def solution(mesh):
    placed = (
        P("seq", None),
        P("seq", "head"),
        P("seq", "head"),
        P("seq", "head"),
        P("head", None),
    ) + (P(),) * 10
    return jax.shard_map(
        local,
        mesh=mesh,
        in_specs=placed,
        out_specs=(P("seq", "head"), P(("seq", "head"), None)),
        check_vma=False,
    )
```
